256 devices in a mesh: dp: 16 (over x, z_lo), tm: 16 (over y, z_hi, core).
Axes of the slice: x: 4, y: 4, z: 8 (z_hi: 2, z_lo: 4; z = z_hi * 4 + z_lo), core: 2. Of those that a mesh axis runs over, the one named last changes fastest.
Arguments:
- frames: bfloat16 [16, 2048, 1536], P('dp', 'tm'), may hold values from -3 to 3
- query: bfloat16 [16, 2048, 1536], P('dp', 'tm'), may hold values from -6 to 6
- keys: bfloat16 [16, 2048, 1536], P('dp', 'tm'), may hold values from -6 to 6
- values: bfloat16 [16, 2048, 1536], P('dp', 'tm'), may hold values from -6 to 6
- norm_gain: float32 [1536], replicated, may hold values from 0.1 to 1.9
- conv_gain: float32 [1536], replicated, may hold values from 0.1 to 1.9
- w_glu: bfloat16 [1536, 3072], P('tm'), may hold values from -0.15625 to 0.15625
- taps: float32 [32, 1536], replicated, may hold values from -1 to 1
- w_out: bfloat16 [1536, 1536], P('tm'), may hold values from -0.15625 to 0.15625
- cotangent: bfloat16 [16, 2048, 1536], P('dp', 'tm'), may hold values from -0.03125 to 0.03125
Outputs:
- glu_grad: float32 [1536, 3072], P('tm')
- taps_grad: float32 [32, 1536], P(None, 'tm')
- out_grad: float32 [1536, 1536], P('tm')
The draws below stay inside these ranges and needn't reach their ends.
All inputs are finite; a program needn't handle non-finite values.
Results may differ from the reference program's by a relative error of at most 0.02.
Values may be sent and summed in bfloat16 or wider, within the bound.
A program may use at most 128 MiB of HBM per device.

```python
import jax
import jax.numpy as jnp
from jax import lax

D = 1536
HEADS = 16
FF2 = 3072
KERNEL = 32
TOK_DEV = 128
HEAD_DIM = 96
LENGTH = 2048
SEQS = 16
N_TM = 16


def drawn_pair(key):
    base = jax.random.fold_in(key, 11)
    first, second = jax.random.split(base, 2)
    shape = (SEQS, LENGTH, D)
    query = jnp.clip(jax.random.normal(first, shape, jnp.float32), -6.0, 6.0)
    keys = jnp.clip(2.0 * jax.random.normal(second, shape, jnp.float32), -6.0, 6.0)
    return (query, keys)


def draw_query(key, part):
    return drawn_pair(key)[0].astype(jnp.bfloat16)


def draw_keys(key, part):
    return drawn_pair(key)[1].astype(jnp.bfloat16)


def block_levels(key, extent, shards, smallest, largest):
    gain = 1.0
    for dim, parts in shards:
        steps = jax.random.uniform(jax.random.fold_in(jax.random.fold_in(key, 6), dim), (parts,), jnp.float32, smallest / len(shards), largest / len(shards))
        gain = gain * jnp.repeat(jnp.exp(steps), extent[dim] // parts).reshape((-1,) + (1,) * (len(extent) - 1 - dim))
    return gain


def noise(key, extent, spread, limit, shards=(), held_as=jnp.bfloat16):
    values = jax.random.normal(key, extent, jnp.float32) * spread
    if len(shards) > 0:
        values = block_levels(key, extent, shards, -0.22, 0.18) * values
    return jnp.clip(values, min=-limit, max=limit).astype(held_as)


def setup_inputs(seed: int = 0) -> dict:
    splits = jax.random.split(jax.random.key(seed), 11)
    frames = noise(splits[0], (SEQS, LENGTH, D), 0.5, 3.0, ((0, 16), (1, 16)))
    query = draw_query(jax.random.fold_in(splits[10], 71), 0)
    keys = draw_keys(jax.random.fold_in(splits[10], 71), 0)
    values = noise(splits[3], (SEQS, LENGTH, D), 1.0, 6.0, ((0, 16), (1, 16)))
    norm_gain = jnp.clip(1.0 + 0.18 * jax.random.normal(splits[4], (D,), jnp.float32), 0.1, 1.9)
    conv_gain = jnp.clip(1.0 + 0.18 * jax.random.normal(splits[5], (D,), jnp.float32), 0.1, 1.9)
    w_glu = noise(splits[6], (D, FF2), D ** -0.5, 0.15625, ((0, 16),))
    taps = noise(splits[7], (KERNEL, D), KERNEL ** -0.5, 1.0, (), jnp.float32)
    w_out = noise(splits[8], (D, D), D ** -0.5, 0.15625, ((0, 16),))
    cotangent = noise(splits[9], (SEQS, LENGTH, D), (SEQS * LENGTH) ** -0.5, 0.03125, ((0, 16), (1, 16)))
    return {"frames": frames, "query": query, "keys": keys, "values": values, "norm_gain": norm_gain, "conv_gain": conv_gain, "w_glu": w_glu, "taps": taps, "w_out": w_out, "cotangent": cotangent}


def standard(v):
    mean = lax.optimization_barrier(jnp.mean(v, axis=-1, keepdims=True))
    centred = v - mean
    var = lax.optimization_barrier(jnp.mean(centred * centred, axis=-1, keepdims=True))
    inv = lax.rsqrt(var + 1e-05)
    return (centred * inv, inv)

def attend(query, keys, values):
    length = query.shape[0]
    stacked = jnp.stack([query, keys, values]).reshape(3, length, HEADS, HEAD_DIM)
    stacked = stacked.transpose(2, 0, 1, 3)

    def one_head(trio):
        scores = jnp.dot(trio[0], trio[1].T, preferred_element_type=jnp.float32) * HEAD_DIM ** (-0.5)
        top = lax.optimization_barrier(jnp.max(scores, axis=1, keepdims=True))
        expo = jnp.exp(scores - top)
        total = lax.optimization_barrier(jnp.sum(expo, axis=1, keepdims=True))
        weights = expo.astype(jnp.bfloat16)
        return (jnp.dot(weights, trio[2], preferred_element_type=jnp.float32) / total).astype(jnp.bfloat16)
    heads_out = lax.map(one_head, stacked)
    return heads_out.transpose(1, 0, 2).reshape(length, D)

def rounded(value):
    return lax.optimization_barrier(value.astype(jnp.bfloat16)).astype(jnp.float32)

def utterance(carry, inputs, norm_gain, conv_gain, w_glu, taps, w_out):
    frames, query, keys, values, cotangent = inputs
    half = KERNEL // 2
    attention = attend(query, keys, values)
    mixed = frames.astype(jnp.float32) + attention.astype(jnp.float32)
    normed, unused = standard(mixed)
    u_rows = (normed * norm_gain).astype(jnp.bfloat16)
    p_full = jnp.dot(u_rows, w_glu, preferred_element_type=jnp.float32)
    first = p_full[:, :D]
    sig = jax.nn.sigmoid(p_full[:, D:])
    y_rows = (first * sig).astype(jnp.bfloat16)
    padded = jnp.pad(y_rows, ((half, half), (0, 0)))
    z_rows = jnp.zeros((LENGTH, D), jnp.float32)
    for k in range(KERNEL):
        z_rows = z_rows + taps[k] * padded[k:k + LENGTH].astype(jnp.float32)
    zhat, inv = standard(z_rows)
    n_rows = zhat * conv_gain
    sgate = jax.nn.sigmoid(n_rows)
    s_rows = (n_rows * sgate).astype(jnp.bfloat16)
    d_s = jnp.dot(cotangent, w_out.T, preferred_element_type=jnp.float32)
    d_n = d_s * sgate * (1.0 + n_rows * (1.0 - sgate))
    e_rows = d_n * conv_gain
    d_z = ((e_rows - lax.optimization_barrier(jnp.mean(e_rows, axis=-1, keepdims=True)) - zhat * lax.optimization_barrier(jnp.mean(e_rows * zhat, axis=-1, keepdims=True))) * inv).astype(jnp.bfloat16)
    dz_pad = jnp.pad(d_z, ((half, half), (0, 0)))
    d_y = jnp.zeros((LENGTH, D), jnp.float32)
    for k in range(KERNEL):
        d_y = d_y + taps[k] * dz_pad[2 * half - k:2 * half - k + LENGTH].astype(jnp.float32)
    d_p = jnp.concatenate([d_y * sig, d_y * first * sig * (1.0 - sig)], axis=1).astype(jnp.bfloat16)

    def block(totals, index):
        start = (index * TOK_DEV).astype(jnp.int32)
        u_b = lax.dynamic_slice_in_dim(u_rows, start, TOK_DEV, 0)
        p_b = lax.dynamic_slice_in_dim(d_p, start, TOK_DEV, 0)
        s_b = lax.dynamic_slice_in_dim(s_rows, start, TOK_DEV, 0)
        c_b = lax.dynamic_slice_in_dim(cotangent, start, TOK_DEV, 0)
        z_b = lax.dynamic_slice_in_dim(d_z, start, TOK_DEV, 0).astype(jnp.float32)
        glu_part = jnp.dot(u_b.T, p_b, preferred_element_type=jnp.float32)
        out_part = jnp.dot(s_b.T, c_b, preferred_element_type=jnp.float32)
        taps_part = jnp.stack([lax.optimization_barrier(jnp.sum(z_b * lax.dynamic_slice_in_dim(padded, start + k, TOK_DEV, 0).astype(jnp.float32), axis=0)) for k in range(KERNEL)])
        return ((totals[0] + rounded(glu_part), totals[1] + rounded(taps_part), totals[2] + rounded(out_part)), None)
    carry, unused_out = lax.scan(block, carry, jnp.arange(N_TM, dtype=jnp.int32))
    return (carry, None)

def reference(frames, query, keys, values, norm_gain, conv_gain, w_glu, taps, w_out, cotangent):
    start_sums = (jnp.zeros((D, FF2), jnp.float32), jnp.zeros((KERNEL, D), jnp.float32), jnp.zeros((D, D), jnp.float32))

    def step(carry, inputs):
        return utterance(carry, inputs, norm_gain, conv_gain, w_glu, taps, w_out)
    sums, unused = lax.scan(step, start_sums, (frames, query, keys, values, cotangent))
    return (sums[0], sums[1], sums[2])
```

```python
import functools

import jax
import jax.numpy as jnp
from jax import lax
from jax.experimental import pallas as pl
from jax.experimental.pallas import tpu as pltpu
from jax.sharding import PartitionSpec as P

N = 16
HD = 96
MESH = pl.DeviceIdType.MESH
F32 = jnp.float32
BF16 = jnp.bfloat16
EPS = 1e-05
TAIL = 16


def rem_copy(src, dst, send, recv, peer):
    return pltpu.make_async_remote_copy(
        src_ref=src, dst_ref=dst, send_sem=send, recv_sem=recv, device_id=peer, device_id_type=MESH
    )


def tm_barrier(me):
    barrier = pltpu.get_barrier_semaphore()
    for i in range(1, N):
        pl.semaphore_signal(
            barrier, inc=1, device_id={"tm": lax.rem(me + i, N)}, device_id_type=MESH
        )
    pl.semaphore_wait(barrier, N - 1)


class Gather:
    def __init__(self, me, own, out, send, recv, local):
        self.own, self.out, self.send, self.recv, self.local = own, out, send, recv, local
        y = me // 4
        z = lax.rem(me // 2, 2)
        c = lax.rem(me, 2)
        at = lambda yy, zz, cc: lax.rem(yy, 4) * 4 + zz * 2 + cc
        self.me = me
        self.far = at(y, 1 - z, c)
        self.sib = at(y, z, 1 - c)
        self.to = [at(y + j, z, c) for j in range(1, 4)]
        self.frm = [at(y + 4 - j, z, c) for j in range(1, 4)]
        self.frm_far = [at(y + 4 - j, 1 - z, c) for j in range(1, 4)]
        self.frm_sib = (
            [self.sib, at(y, 1 - z, 1 - c)]
            + [at(y + 4 - j, z, 1 - c) for j in range(1, 4)]
            + [at(y + 4 - j, 1 - z, 1 - c) for j in range(1, 4)]
        )
        self.started = []

    def go(self, src, slot, sem, peer):
        copy = rem_copy(
            src, self.out.at[slot], self.send.at[sem], self.recv.at[sem], {"tm": peer}
        )
        copy.start()
        self.started.append(copy)

    def landed(self, slot, sem):
        ref = self.out.at[slot]
        rem_copy(ref, ref, self.send.at[sem], self.recv.at[sem], {"tm": self.sib}).wait_recv()

    def start(self):
        self.keep = pltpu.make_async_copy(self.own, self.out.at[self.me], self.local)
        self.go(self.own, self.me, 0, self.far)
        for j in range(3):
            self.go(self.own, self.me, 1 + j, self.to[j])
        self.go(self.own, self.me, 7, self.sib)
        self.keep.start()

    def relay_far(self):
        self.landed(self.far, 0)
        for j in range(3):
            self.go(self.out.at[self.far], self.far, 4 + j, self.to[j])
        self.go(self.out.at[self.far], self.far, 8, self.sib)

    def relay_near(self):
        for j in (0, 2, 1):
            self.landed(self.frm[j], 1 + j)
            self.go(self.out.at[self.frm[j]], self.frm[j], 9 + j, self.sib)

    def relay_rest(self):
        for j in (0, 2, 1):
            self.landed(self.frm_far[j], 4 + j)
            self.go(self.out.at[self.frm_far[j]], self.frm_far[j], 12 + j, self.sib)

    def finish(self):
        for k in range(8):
            self.landed(self.frm_sib[k], 7 + k)
        for copy in self.started:
            copy.wait_send()
        self.keep.wait()


class Swap:
    def __init__(self, me, buf, send, recv):
        self.me, self.buf, self.send, self.recv = me, buf, send, recv
        self.started = []

    def start(self):
        for i in range(1, N):
            copy = rem_copy(
                self.buf.at[self.me],
                self.buf.at[self.me],
                self.send.at[i],
                self.recv.at[i],
                {"tm": lax.rem(self.me + i, N)},
            )
            copy.start()
            self.started.append(copy)

    def finish(self):
        for i in range(1, N):
            ref = self.buf.at[lax.rem(self.me + N - i, N)]
            rem_copy(ref, ref, self.send.at[i], self.recv.at[i], {"tm": self.me}).wait_recv()
        for copy in self.started:
            copy.wait_send()


def own_stats(x):
    mean = jnp.mean(x, axis=0, keepdims=True)
    dev = x - mean
    return mean, jnp.sum(dev * dev, axis=0, keepdims=True)


def joined_stats(buf):
    means = buf[:, 0, :]
    squares = buf[:, 1, :]
    mean = jnp.mean(means, axis=0, keepdims=True)
    dev = means - mean
    total = jnp.sum(squares, axis=0, keepdims=True) + HD * jnp.sum(dev * dev, axis=0, keepdims=True)
    return mean, lax.rsqrt(total * (1.0 / (N * HD)) + EPS)


def front_kernel(
    q_ref, k_ref, v_ref, f_ref, w_ref, cot_ref, gain_ref,
    u_out, cot_out, w_out,
    packed, got, k_rows, v_cols, mixed, stats, own_u,
    x_send, x_recv, w_send, w_recv, s_send, s_recv, c_send, c_recv, u_send, u_recv, keep_sem,
):
    me = lax.axis_index("tm")
    length = mixed.shape[1]
    rows = q_ref.shape[0]
    for a, ref in enumerate((k_ref, v_ref, q_ref, f_ref)):
        turned = jnp.transpose(ref[...])
        for d in range(N):
            packed[d, a * HD : (a + 1) * HD, :] = turned[d * HD : (d + 1) * HD]
    tm_barrier(me)
    cot = Gather(me, cot_ref, cot_out, c_send, c_recv, keep_sem.at[0])
    x_copies, w_copies = [], []
    for i in range(1, N):
        peer = lax.rem(me + i, N)
        copy = rem_copy(packed.at[peer], got.at[me], x_send.at[i], x_recv.at[i], {"tm": peer})
        copy.start()
        x_copies.append(copy)
    cot.start()
    for i in range(1, N):
        peer = lax.rem(me + i, N)
        copy = rem_copy(w_ref.at[peer], w_out.at[me], w_send.at[i], w_recv.at[i], {"tm": peer})
        copy.start()
        w_copies.append(copy)
    w_keep = pltpu.make_async_copy(w_ref.at[me], w_out.at[me], keep_sem.at[1])
    w_keep.start()
    got[me] = packed[me]
    for i in range(1, N):
        ref = got.at[lax.rem(me + N - i, N)]
        rem_copy(ref, ref, x_send.at[i], x_recv.at[i], {"tm": me}).wait_recv()
    for s in range(N):
        k_rows[s * rows : (s + 1) * rows, :] = jnp.transpose(got[s, 0:HD, :])
        v_cols[:, s * rows : (s + 1) * rows] = got[s, HD : 2 * HD, :]
    cot.relay_far()

    factor = HD ** -0.5 * 1.4426950408889634
    pair = 2

    def attend(i):
        queries = jnp.concatenate(
            [got[i * pair + j, 2 * HD : 3 * HD, :] for j in range(pair)], axis=1
        )
        field = jnp.concatenate(
            [got[i * pair + j, 3 * HD : 4 * HD, :] for j in range(pair)], axis=1
        )
        scores = jnp.dot(k_rows[...], queries, preferred_element_type=F32)
        top = jnp.max(scores, axis=0, keepdims=True)
        expo = jnp.exp2(scores * factor - top * factor)
        total = jnp.sum(expo, axis=0, keepdims=True)
        summed = jnp.dot(v_cols[...], expo.astype(BF16), preferred_element_type=F32)
        attention = (summed / total).astype(BF16)
        block = field.astype(F32) + attention.astype(F32)
        cols = pl.ds(pl.multiple_of(i * pair * rows, pair * rows), pair * rows)
        mixed[:, cols] = block
        mean, square = own_stats(block)
        stats[me, 0:1, cols] = mean
        stats[me, 1:2, cols] = square

    half = N // pair // 2

    @pl.loop(0, half)
    def first(i):
        attend(i)

    cot.relay_near()

    @pl.loop(half, 2 * half)
    def second(i):
        attend(i)

    swap = Swap(me, stats, s_send, s_recv)
    swap.start()
    cot.relay_rest()
    swap.finish()
    mean, inv = joined_stats(stats)
    own_u[...] = ((mixed[...] - mean) * inv * gain_ref[...]).astype(BF16)
    ug = Gather(me, own_u, u_out, u_send, u_recv, keep_sem.at[2])
    ug.start()
    ug.relay_far()
    ug.relay_near()
    ug.relay_rest()
    cot.finish()
    for i in range(1, N):
        ref = w_out.at[lax.rem(me + N - i, N)]
        rem_copy(ref, ref, w_send.at[i], w_recv.at[i], {"tm": me}).wait_recv()
    for copy in x_copies + w_copies:
        copy.wait_send()
    w_keep.wait()
    ug.finish()


def vmem():
    return pl.BlockSpec(memory_space=pltpu.VMEM)


def anywhere():
    return pl.BlockSpec(memory_space=pl.ANY)


def front(query, keys, values, frames, w_parts, cot, gain):
    rows, width = query.shape
    length = rows * N
    dma = pltpu.SemaphoreType.DMA
    return pl.pallas_call(
        front_kernel,
        out_shape=(
            jax.ShapeDtypeStruct((N, HD, length), BF16),
            jax.ShapeDtypeStruct((N, rows, width), BF16),
            jax.ShapeDtypeStruct(w_parts.shape, BF16),
        ),
        in_specs=[vmem(), vmem(), vmem(), vmem(), anywhere(), anywhere(), vmem()],
        out_specs=(anywhere(), anywhere(), anywhere()),
        scratch_shapes=[
            pltpu.VMEM((N, 4 * HD, rows), BF16),
            pltpu.VMEM((N, 4 * HD, rows), BF16),
            pltpu.VMEM((length, HD), BF16),
            pltpu.VMEM((HD, length), BF16),
            pltpu.VMEM((HD, length), F32),
            pltpu.VMEM((N, 2, length), F32),
            pltpu.VMEM((HD, length), BF16),
            dma((N,)), dma((N,)), dma((N,)), dma((N,)), dma((N,)), dma((N,)),
            dma((15,)), dma((15,)), dma((15,)), dma((15,)), dma((3,)),
        ],
        compiler_params=pltpu.CompilerParams(
            collective_id=0, has_side_effects=True, vmem_limit_bytes=56 * 2**20
        ),
        name="front",
    )(query, keys, values, frames, w_parts, cot, gain)


def middle_kernel(
    p_ref, ds_ref, taps_ref, gain_ref,
    dp_out, s_out, taps_out,
    y_pad, z_cols, g_cols, dz_pad, stats, stats_e,
    s_send, s_recv, e_send, e_recv,
):
    me = lax.axis_index("tm")
    length = z_cols.shape[1]
    kernel = taps_ref.shape[0]
    half = kernel // 2
    step = 128
    blocks = length // step
    lanes = y_pad.shape[1]
    blank = jnp.zeros((lanes - HD, step), F32)

    edge = jnp.zeros((half, lanes), F32)
    for pad in (y_pad, dz_pad):
        pad[0:half, :] = edge
        pad[length + half : length + 2 * half, :] = edge

    @pl.loop(0, blocks)
    def gate(i):
        cols = pl.ds(pl.multiple_of(i * step, step), step)
        y = p_ref[0:HD, cols] * jax.nn.sigmoid(p_ref[HD : 2 * HD, cols])
        y = y.astype(BF16).astype(F32)
        y_pad[pl.ds(pl.multiple_of(half + i * step, half), step), :] = jnp.transpose(
            jnp.concatenate([y, blank], axis=0)
        )

    @pl.loop(0, blocks)
    def conv(i):
        start = pl.multiple_of(i * step, step)
        z = jnp.zeros((step, lanes), F32)
        for k in range(kernel):
            z = z + taps_ref[k : k + 1, :] * y_pad[pl.ds(start + k, step), :]
        z = jnp.transpose(z)[0:HD]
        cols = pl.ds(start, step)
        z_cols[:, cols] = z
        mean, square = own_stats(z)
        stats[me, 0:1, cols] = mean
        stats[me, 1:2, cols] = square

    tm_barrier(me)
    swap = Swap(me, stats, s_send, s_recv)
    swap.start()
    swap.finish()
    mean, inv = joined_stats(stats)
    gain = gain_ref[...]
    zhat = (z_cols[...] - mean) * inv
    z_cols[...] = zhat
    n = zhat * gain
    sgate = jax.nn.sigmoid(n)
    s_out[...] = (n * sgate).astype(BF16)
    e = ds_ref[...] * sgate * (1.0 + n * (1.0 - sgate)) * gain
    g_cols[...] = e
    stats_e[me, 0:1, :] = jnp.sum(e, axis=0, keepdims=True)
    stats_e[me, 1:2, :] = jnp.sum(e * zhat, axis=0, keepdims=True)
    swap_e = Swap(me, stats_e, e_send, e_recv)
    swap_e.start()
    swap_e.finish()
    sums = jnp.sum(stats_e[...], axis=0) * (1.0 / (N * HD))
    g_cols[...] = (
        ((g_cols[...] - sums[0:1] - z_cols[...] * sums[1:2]) * inv).astype(BF16).astype(F32)
    )

    @pl.loop(0, blocks)
    def turn(i):
        cols = pl.ds(pl.multiple_of(i * step, step), step)
        dz_pad[pl.ds(pl.multiple_of(half + i * step, half), step), :] = jnp.transpose(
            jnp.concatenate([g_cols[:, cols], blank], axis=0)
        )

    taps_out[...] = jnp.zeros_like(taps_out)

    @pl.loop(0, blocks)
    def back(i):
        start = pl.multiple_of(i * step, step)
        dy = jnp.zeros((step, lanes), F32)
        for k in range(kernel):
            dy = dy + taps_ref[k : k + 1, :] * dz_pad[pl.ds(start + 2 * half - k, step), :]
        dy = jnp.transpose(dy)[0:HD]
        cols = pl.ds(start, step)
        pa = p_ref[0:HD, cols]
        sig = jax.nn.sigmoid(p_ref[HD : 2 * HD, cols])
        dp_out[0:HD, cols] = (dy * sig).astype(BF16)
        dp_out[HD : 2 * HD, cols] = (dy * pa * sig * (1.0 - sig)).astype(BF16)
        dz = dz_pad[pl.ds(pl.multiple_of(half + start, half), step), :]
        for k in range(kernel):
            prod = dz * y_pad[pl.ds(start + k, step), :]
            taps_out[k : k + 1, :] += jnp.sum(prod, axis=0, keepdims=True)


def middle(p_cols, ds_cols, taps, gain):
    length = p_cols.shape[1]
    kernel, lanes = taps.shape
    dma = pltpu.SemaphoreType.DMA
    return pl.pallas_call(
        middle_kernel,
        out_shape=(
            jax.ShapeDtypeStruct((2 * HD, length), BF16),
            jax.ShapeDtypeStruct((HD, length), BF16),
            jax.ShapeDtypeStruct((kernel, lanes), F32),
        ),
        in_specs=[vmem()] * 4,
        out_specs=(vmem(), vmem(), vmem()),
        scratch_shapes=[
            pltpu.VMEM((length + kernel, lanes), F32),
            pltpu.VMEM((HD, length), F32),
            pltpu.VMEM((HD, length), F32),
            pltpu.VMEM((length + kernel, lanes), F32),
            pltpu.VMEM((N, 2, length), F32),
            pltpu.VMEM((N, 2, length), F32),
            dma((N,)), dma((N,)), dma((N,)), dma((N,)),
        ],
        compiler_params=pltpu.CompilerParams(
            collective_id=1, has_side_effects=True, vmem_limit_bytes=56 * 2**20
        ),
        name="middle",
    )(p_cols, ds_cols, taps, gain)


def reduce_kernel(
    g_ref, o_ref, t_ref, g_out, o_out, t_out,
    g_got, o_got, t_got, g_red, o_red,
    gs, gr, os, orr, ts, tr, g2s, g2r, o2s, o2r,
):
    d = lax.axis_index("dp")
    t = lax.axis_index("tm")
    barrier = pltpu.get_barrier_semaphore()

    def greet(dp, tm):
        pl.semaphore_signal(
            barrier, inc=1, device_id={"dp": dp, "tm": tm}, device_id_type=MESH
        )

    for i in range(1, N):
        peer = lax.rem(d + i, N)
        greet(peer, t)
        greet(peer, d)
        greet(t, lax.rem(t + i, N))

    @pl.when(t != d)
    def _():
        greet(d, d)
        greet(t, t)

    pl.semaphore_wait(barrier, jnp.where(t == d, 3 * (N - 1), 3 * (N - 1) + 2))

    first = []
    for i in range(1, N):
        peer = lax.rem(d + i, N)
        to = {"dp": peer, "tm": t}
        first.append(rem_copy(g_ref.at[peer], g_got.at[d], gs.at[i], gr.at[i], to))
        first.append(rem_copy(o_ref.at[peer], o_got.at[d], os.at[i], orr.at[i], to))
        first.append(rem_copy(t_ref, t_got.at[d], ts.at[i], tr.at[i], to))
        for copy in first[-3:]:
            copy.start()
    g_got[d] = g_ref[d]
    o_got[d] = o_ref[d]
    t_got[d] = t_ref[...]
    here = {"dp": d, "tm": t}
    for i in range(1, N):
        slot = lax.rem(d + N - i, N)
        for buf, send, recv in ((g_got, gs, gr), (o_got, os, orr), (t_got, ts, tr)):
            rem_copy(buf.at[slot], buf.at[slot], send.at[i], recv.at[i], here).wait_recv()
    g_red[...] = jnp.sum(g_got[...].astype(F32), axis=0).astype(BF16)
    o_red[...] = jnp.sum(o_got[...].astype(F32), axis=0).astype(BF16)
    t_out[...] = jnp.sum(t_got[...].astype(F32), axis=0)

    second = []
    for i in range(1, N):
        peer = lax.rem(d + i, N)
        second.append(
            rem_copy(g_red, g_out.at[t], g2s.at[i], g2r.at[t], {"dp": peer, "tm": d})
        )
        second.append(
            rem_copy(o_red, o_out.at[d], o2s.at[i], o2r.at[i], {"dp": peer, "tm": t})
        )
        second[-2].start()
        second[-1].start()
    last = rem_copy(g_red, g_out.at[t], g2s.at[0], g2r.at[t], {"dp": d, "tm": d})

    @pl.when(t != d)
    def _():
        last.start()

    @pl.when(t == d)
    def _():
        g_out[t] = g_red[...]

    o_out[d] = o_red[...]
    for i in range(1, N):
        slot = lax.rem(d + N - i, N)
        ref = o_out.at[slot]
        rem_copy(ref, ref, o2s.at[i], o2r.at[i], here).wait_recv()
        slot = lax.rem(t + i, N)
        ref = g_out.at[slot]
        rem_copy(ref, ref, g2s.at[i], g2r.at[slot], here).wait_recv()

    @pl.when(t != d)
    def _():
        ref = g_out.at[t]
        rem_copy(ref, ref, g2s.at[0], g2r.at[t], here).wait_recv()
        last.wait_send()

    for copy in first + second:
        copy.wait_send()


def reduce_all(g_parts, o_parts, t_part):
    dma = pltpu.SemaphoreType.DMA
    return pl.pallas_call(
        reduce_kernel,
        out_shape=(
            jax.ShapeDtypeStruct(g_parts.shape, BF16),
            jax.ShapeDtypeStruct(o_parts.shape, BF16),
            jax.ShapeDtypeStruct(t_part.shape, F32),
        ),
        in_specs=[vmem()] * 3,
        out_specs=(vmem(), vmem(), vmem()),
        scratch_shapes=[
            pltpu.VMEM(g_parts.shape, BF16),
            pltpu.VMEM(o_parts.shape, BF16),
            pltpu.VMEM((N,) + t_part.shape, BF16),
            pltpu.VMEM(g_parts.shape[1:], BF16),
            pltpu.VMEM(o_parts.shape[1:], BF16),
        ] + [dma((N,))] * 10,
        compiler_params=pltpu.CompilerParams(
            collective_id=2, has_side_effects=True, vmem_limit_bytes=56 * 2**20
        ),
        name="reduce_all",
    )(g_parts, o_parts, t_part)


def local(frames, query, keys, values, norm_gain, conv_gain, w_glu, taps, w_out, cotangent):
    rows, width = frames.shape[1:]
    length = rows * N
    t = lax.axis_index("tm")
    own = lambda gain: lax.dynamic_slice_in_dim(gain, t * HD, HD).reshape(HD, 1)
    w_parts = w_glu.reshape(HD, 2, N, HD).transpose(2, 0, 1, 3).reshape(N, HD, 2 * HD)
    u_all, cot_all, w_cols = front(
        query[0], keys[0], values[0], frames[0], w_parts, cotangent[0], own(norm_gain)
    )
    u_cols = u_all.reshape(width, length)
    cot_rows = cot_all.reshape(length, width)
    p_cols = lax.dot_general(
        w_cols.reshape(width, 2 * HD), u_cols, (((0,), (0,)), ((), ())), preferred_element_type=F32
    )
    ds_cols = lax.dot_general(
        w_out, cot_rows, (((1,), (1,)), ((), ())), preferred_element_type=F32
    )
    own_taps = jnp.pad(lax.dynamic_slice_in_dim(taps, t * HD, HD, axis=1), ((0, 0), (0, 128 - HD)))
    dp_cols, s_cols, taps_part = middle(p_cols, ds_cols, own_taps, own(conv_gain))
    g_part = lax.dot_general(
        u_cols, dp_cols, (((1,), (1,)), ((), ())), preferred_element_type=F32
    ).astype(BF16)
    o_part = lax.dot_general(
        s_cols, cot_rows, (((1,), (0,)), ((), ())), preferred_element_type=F32
    ).astype(BF16)
    g_all, o_all, t_all = reduce_all(
        g_part.reshape(N, HD, 2 * HD),
        o_part.reshape(HD, N, HD).transpose(1, 0, 2),
        taps_part.astype(BF16),
    )
    glu_grad = g_all.reshape(N, HD, 2, HD).transpose(1, 2, 0, 3).reshape(HD, 2 * width).astype(F32)
    out_grad = o_all.transpose(1, 0, 2).reshape(HD, width).astype(F32)
    return glu_grad, t_all[:, :HD], out_grad


def solution(mesh):
    return jax.shard_map(
        local,
        mesh=mesh,
        in_specs=(
            P("dp", "tm", None),
            P("dp", "tm", None),
            P("dp", "tm", None),
            P("dp", "tm", None),
            P(),
            P(),
            P("tm", None),
            P(),
            P("tm", None),
            P("dp", "tm", None),
        ),
        out_specs=(P("tm", None), P(None, "tm"), P("tm", None)),
        check_vma=False,
    )
```

```python
import functools

import jax
import jax.numpy as jnp
from jax import lax
from jax.experimental import pallas as pl
from jax.experimental.pallas import tpu as pltpu
from jax.sharding import PartitionSpec as P

N = 16
HD = 96
MESH = pl.DeviceIdType.MESH
F32 = jnp.float32
BF16 = jnp.bfloat16
EPS = 1e-05


def rem_copy(src, dst, send, recv, peer):
    return pltpu.make_async_remote_copy(
        src_ref=src, dst_ref=dst, send_sem=send, recv_sem=recv, device_id=peer, device_id_type=MESH
    )


class Gather:
    def __init__(self, me, own, out, slot, send, recv):
        self.own, self.out, self.slot, self.send, self.recv = own, out, slot, send, recv
        y = me // 4
        z = lax.rem(me // 2, 2)
        c = lax.rem(me, 2)
        at = lambda yy, zz, cc: lax.rem(yy, 4) * 4 + zz * 2 + cc
        self.me = me
        self.far = at(y, 1 - z, c)
        self.sib = at(y, z, 1 - c)
        self.to = [at(y + j, z, c) for j in range(1, 4)]
        self.frm = [at(y + 4 - j, z, c) for j in range(1, 4)]
        self.frm_far = [at(y + 4 - j, 1 - z, c) for j in range(1, 4)]
        self.frm_sib = (
            [self.sib, at(y, 1 - z, 1 - c)]
            + [at(y + 4 - j, z, 1 - c) for j in range(1, 4)]
            + [at(y + 4 - j, 1 - z, 1 - c) for j in range(1, 4)]
        )
        self.started = []

    def go(self, src, block, sem, peer):
        copy = rem_copy(
            src, self.out.at[self.slot(block)], self.send.at[sem], self.recv.at[sem], {"tm": peer}
        )
        copy.start()
        self.started.append(copy)

    def on(self, block, sem, peer):
        self.go(self.out.at[self.slot(block)], block, sem, peer)

    def landed(self, block, sem):
        ref = self.out.at[self.slot(block)]
        rem_copy(ref, ref, self.send.at[sem], self.recv.at[sem], {"tm": self.sib}).wait_recv()

    def start(self):
        self.go(self.own, self.me, 0, self.far)
        for j in (0, 2, 1):
            self.go(self.own, self.me, 1 + j, self.to[j])
        self.go(self.own, self.me, 7, self.sib)

    def relay_far(self):
        self.landed(self.far, 0)
        for j in (0, 2, 1):
            self.on(self.far, 4 + j, self.to[j])
        self.on(self.far, 8, self.sib)

    def relay_near(self):
        for j in (0, 2, 1):
            self.landed(self.frm[j], 1 + j)
            self.on(self.frm[j], 9 + j, self.sib)

    def relay_rest(self):
        for j in (0, 2, 1):
            self.landed(self.frm_far[j], 4 + j)
            self.on(self.frm_far[j], 12 + j, self.sib)

    def near_from_sibling(self):
        for k in (0, 2, 3, 4):
            self.landed(self.frm_sib[k], 7 + k)

    def rest_from_sibling(self):
        for k in (1, 5, 6, 7):
            self.landed(self.frm_sib[k], 7 + k)

    def sent(self):
        for copy in self.started:
            copy.wait_send()


class Swap:
    def __init__(self, me, buf, send, recv):
        self.me, self.buf, self.send, self.recv = me, buf, send, recv
        self.started = []

    def start(self):
        for i in range(1, N):
            copy = rem_copy(
                self.buf.at[self.me],
                self.buf.at[self.me],
                self.send.at[i],
                self.recv.at[i],
                {"tm": lax.rem(self.me + i, N)},
            )
            copy.start()
            self.started.append(copy)

    def finish(self):
        for i in range(1, N):
            ref = self.buf.at[lax.rem(self.me + N - i, N)]
            rem_copy(ref, ref, self.send.at[i], self.recv.at[i], {"tm": self.me}).wait_recv()
        for copy in self.started:
            copy.wait_send()


def own_stats(x):
    mean = jnp.mean(x, axis=0, keepdims=True)
    dev = x - mean
    return mean, jnp.sum(dev * dev, axis=0, keepdims=True)


def joined_stats(buf):
    means = buf[:, 0, :]
    squares = buf[:, 1, :]
    mean = jnp.mean(means, axis=0, keepdims=True)
    dev = means - mean
    total = jnp.sum(squares, axis=0, keepdims=True) + HD * jnp.sum(dev * dev, axis=0, keepdims=True)
    return mean, lax.rsqrt(total * (1.0 / (N * HD)) + EPS)


def core_kernel(
    q_ref, k_ref, v_ref, f_ref, wg_ref, wo_ref, cot_ref, taps_ref, ng_ref, cg_ref,
    glu_out, out_out, taps_out,
    kv_own, qf_own, kv, qf, k_rows, v_cols, mixed, stats, stats_z, stats_e,
    w_own, w_got, u_all, cot_all, small, taps_own, p, ds, y_pad, dz_pad, z_cols, g_cols, s_cols, dp,
    t_own, g_own, o_own, g_got, o_got, t_got, g_red, o_red, g_fin, o_fin,
    kv_s, kv_r, qf_s, qf_r, w_s, w_r, st_s, st_r, sz_s, sz_r, se_s, se_r,
    c_s, c_r, u_s, u_r, g1_s, g1_r, o1_s, o1_r, t1_s, t1_r, g2_s, g2_r, o2_s, o2_r, own_sem,
):
    d = lax.axis_index("dp")
    t = lax.axis_index("tm")
    rows = q_ref.shape[0]
    length = mixed.shape[1]
    kernel = taps_ref.shape[0]
    half = kernel // 2
    y_at = t // 4
    group = lax.rem(t, 4)
    place = lambda block: lax.rem(block, 4) * 4 + block // 4

    barrier = pltpu.get_barrier_semaphore()

    def greet(dp_at, tm_at):
        pl.semaphore_signal(
            barrier, inc=1, device_id={"dp": dp_at, "tm": tm_at}, device_id_type=MESH
        )

    for i in range(1, N):
        greet(d, lax.rem(t + i, N))
        greet(lax.rem(d + i, N), t)
        greet(lax.rem(d + i, N), d)
        greet(t, lax.rem(t + i, N))

    @pl.when(t != d)
    def _():
        greet(d, d)
        greet(t, t)

    def turn_into(ref, buf, a):
        turned = jnp.transpose(ref[...])
        for j in range(N):
            buf[j, a * HD : (a + 1) * HD, :] = turned[j * HD : (j + 1) * HD]

    sent = []

    def scatter(src, dst, slot, send, recv):
        for i in range(1, N):
            peer = lax.rem(t + i, N)
            copy = rem_copy(src.at[peer], dst.at[slot], send.at[i], recv.at[i], {"tm": peer})
            copy.start()
            sent.append(copy)

    def arrived(dst, slot, i, send, recv):
        ref = dst.at[slot]
        rem_copy(ref, ref, send.at[i], recv.at[i], {"tm": t}).wait_recv()

    turn_into(k_ref, kv_own, 0)
    turn_into(v_ref, kv_own, 1)
    cot_keep = pltpu.make_async_copy(cot_ref, cot_all.at[t], own_sem)
    cot_keep.start()
    pl.semaphore_wait(barrier, jnp.where(t == d, 4 * (N - 1), 4 * (N - 1) + 2))
    scatter(kv_own, kv, t, kv_s, kv_r)
    turn_into(q_ref, qf_own, 0)
    turn_into(f_ref, qf_own, 1)
    scatter(qf_own, qf, t, qf_s, qf_r)
    width = N * HD
    for j in range(N):
        w_own[j] = jnp.concatenate(
            [
                wg_ref[:, j * HD : (j + 1) * HD],
                wg_ref[:, width + j * HD : width + (j + 1) * HD],
            ],
            axis=1,
        )
    scatter(w_own, w_got, place(t), w_s, w_r)
    kv[t] = kv_own[t]
    qf[t] = qf_own[t]
    w_got[place(t)] = w_own[t]

    small[...] = jnp.transpose(
        jnp.concatenate(
            [
                taps_ref[...],
                ng_ref[...],
                cg_ref[...],
                jnp.zeros((128 - kernel - 2, width), F32),
            ],
            axis=0,
        )
    )
    mine = small[pl.ds(pl.multiple_of(t * HD, HD), HD), :]
    lanes = taps_own.shape[1]
    blank = jnp.zeros((lanes - HD, 128), F32)
    taps_own[...] = jnp.transpose(jnp.concatenate([mine, blank], axis=0))[0:kernel]
    norm_gain = mine[:, kernel : kernel + 1]
    conv_gain = mine[:, kernel + 1 : kernel + 2]
    edge = jnp.zeros((half, lanes), F32)
    for pad in (y_pad, dz_pad):
        pad[0:half, :] = edge
        pad[length + half : length + 2 * half, :] = edge

    for i in range(1, N):
        arrived(kv, lax.rem(t + N - i, N), i, kv_s, kv_r)
    for s in range(N):
        k_rows[s * rows : (s + 1) * rows, :] = jnp.transpose(kv[s, 0:HD, :])
        v_cols[:, s * rows : (s + 1) * rows] = kv[s, HD : 2 * HD, :]
    cot = Gather(t, cot_ref, cot_all, lambda block: block, c_s, c_r)
    cot.start()

    factor = HD ** -0.5 * 1.4426950408889634
    pair = 2

    @pl.loop(0, N // pair)
    def attend(i):
        for j in range(pair):
            s = i * pair + j

            @pl.when(s != t)
            def _():
                arrived(qf, s, lax.rem(t + N - s, N), qf_s, qf_r)

        queries = jnp.concatenate([qf[i * pair + j, 0:HD, :] for j in range(pair)], axis=1)
        field = jnp.concatenate([qf[i * pair + j, HD : 2 * HD, :] for j in range(pair)], axis=1)
        scores = jnp.dot(k_rows[...], queries, preferred_element_type=F32)
        top = jnp.max(scores, axis=0, keepdims=True)
        expo = jnp.exp2(scores * factor - top * factor)
        total = jnp.sum(expo, axis=0, keepdims=True)
        summed = jnp.dot(v_cols[...], expo.astype(BF16), preferred_element_type=F32)
        attention = (summed / total).astype(BF16)
        block = field.astype(F32) + attention.astype(F32)
        cols = pl.ds(pl.multiple_of(i * pair * rows, pair * rows), pair * rows)
        mixed[:, cols] = block
        mean, square = own_stats(block)
        stats[t, 0:1, cols] = mean
        stats[t, 1:2, cols] = square

    swap = Swap(t, stats, st_s, st_r)
    swap.start()
    cot.relay_near()
    swap.finish()
    mean, inv = joined_stats(stats)
    u_all[place(t)] = ((mixed[...] - mean) * inv * norm_gain).astype(BF16)
    ug = Gather(t, u_all.at[place(t)], u_all, place, u_s, u_r)
    ug.start()

    def back_rows(z):
        @pl.loop(0, 4)
        def _(yy):
            first = yy * 4 + z * 2
            block = cot_all[pl.ds(first, 2)].reshape(2 * rows, width)
            ds[:, pl.ds(pl.multiple_of(first * rows, 2 * rows), 2 * rows)] = lax.dot_general(
                wo_ref[...], block, (((1,), (1,)), ((), ())), preferred_element_type=F32
            )

    z_at = lax.rem(t // 2, 2)
    cot.near_from_sibling()
    cot_keep.wait()
    back_rows(z_at)

    for i in range(1, N):
        arrived(w_got, place(lax.rem(t + N - i, N)), i, w_s, w_r)
    chunk = 512

    def product(g, first):
        weights = w_got[pl.ds(g * 4, 4)].reshape(4 * HD, 2 * HD)

        @pl.loop(0, length // chunk)
        def _(i):
            cols = pl.ds(pl.multiple_of(i * chunk, chunk), chunk)
            part = u_all[pl.ds(g * 4, 4), :, cols].reshape(4 * HD, chunk)
            part = lax.dot_general(
                weights, part, (((0,), (0,)), ((), ())), preferred_element_type=F32
            )
            p[:, cols] = part if first else p[:, cols] + part

    side = lax.rem(group + 1, 2) - lax.rem(group, 2)
    ug.relay_far()
    ug.relay_near()
    product(group, True)
    ug.near_from_sibling()
    product(group + side, False)
    ug.relay_rest()
    cot.relay_far()
    other = lax.rem(group + 2, 4)
    product(other, False)
    ug.rest_from_sibling()
    product(other + side, False)

    step = 128
    blocks = length // step

    @pl.loop(0, blocks)
    def gate(i):
        cols = pl.ds(pl.multiple_of(i * step, step), step)
        y = p[0:HD, cols] * jax.nn.sigmoid(p[HD : 2 * HD, cols])
        y = y.astype(BF16).astype(F32)
        y_pad[pl.ds(pl.multiple_of(half + i * step, half), step), :] = jnp.transpose(
            jnp.concatenate([y, blank], axis=0)
        )

    @pl.loop(0, blocks)
    def conv(i):
        start = pl.multiple_of(i * step, step)
        z = jnp.zeros((step, lanes), F32)
        for k in range(kernel):
            z = z + taps_own[k : k + 1, :] * y_pad[pl.ds(start + k, step), :]
        z = jnp.transpose(z)[0:HD]
        cols = pl.ds(start, step)
        z_cols[:, cols] = z
        mean, square = own_stats(z)
        stats_z[t, 0:1, cols] = mean
        stats_z[t, 1:2, cols] = square

    swap = Swap(t, stats_z, sz_s, sz_r)
    swap.start()
    cot.relay_rest()
    cot.rest_from_sibling()
    back_rows(1 - z_at)
    swap.finish()
    mean, inv = joined_stats(stats_z)
    zhat = (z_cols[...] - mean) * inv
    z_cols[...] = zhat
    n = zhat * conv_gain
    sgate = jax.nn.sigmoid(n)
    s_cols[...] = (n * sgate).astype(BF16)
    e = ds[...] * sgate * (1.0 + n * (1.0 - sgate)) * conv_gain
    g_cols[...] = e
    stats_e[t, 0:1, :] = jnp.sum(e, axis=0, keepdims=True)
    stats_e[t, 1:2, :] = jnp.sum(e * zhat, axis=0, keepdims=True)
    swap_e = Swap(t, stats_e, se_s, se_r)
    swap_e.start()

    for j in range(4):
        cols = slice(j * 4 * HD, (j + 1) * 4 * HD)
        part = jnp.dot(
            s_cols[...], cot_all[:, :, cols].reshape(length, 4 * HD), preferred_element_type=F32
        ).astype(BF16)
        for k in range(4):
            o_own[4 * j + k] = part[:, k * HD : (k + 1) * HD]
    for i in range(1, N):
        peer = lax.rem(d + i, N)
        copy = rem_copy(o_own.at[peer], o_got.at[d], o1_s.at[i], o1_r.at[i], {"dp": peer, "tm": t})
        copy.start()
        sent.append(copy)
    o_got[d] = o_own[d]

    swap_e.finish()
    sums = jnp.sum(stats_e[...], axis=0) * (1.0 / (N * HD))
    g_cols[...] = (
        ((g_cols[...] - sums[0:1] - z_cols[...] * sums[1:2]) * inv).astype(BF16).astype(F32)
    )

    @pl.loop(0, blocks)
    def turn(i):
        cols = pl.ds(pl.multiple_of(i * step, step), step)
        dz_pad[pl.ds(pl.multiple_of(half + i * step, half), step), :] = jnp.transpose(
            jnp.concatenate([g_cols[:, cols], blank], axis=0)
        )

    t_own[...] = jnp.zeros_like(t_own)

    @pl.loop(0, blocks)
    def back(i):
        start = pl.multiple_of(i * step, step)
        dy = jnp.zeros((step, lanes), F32)
        for k in range(kernel):
            dy = dy + taps_own[k : k + 1, :] * dz_pad[pl.ds(start + 2 * half - k, step), :]
        dy = jnp.transpose(dy)[0:HD]
        cols = pl.ds(start, step)
        pa = p[0:HD, cols]
        sig = jax.nn.sigmoid(p[HD : 2 * HD, cols])
        dp[0:HD, cols] = (dy * sig).astype(BF16)
        dp[HD : 2 * HD, cols] = (dy * pa * sig * (1.0 - sig)).astype(BF16)
        dz = dz_pad[pl.ds(pl.multiple_of(half + start, half), step), :]
        for k in range(kernel):
            prod = dz * y_pad[pl.ds(start + k, step), :]
            t_own[k : k + 1, :] += jnp.sum(prod, axis=0, keepdims=True)

    @pl.loop(0, 4)
    def grads(i):
        g = lax.rem(i + d, 4)
        part = lax.dot_general(
            u_all[pl.ds(g * 4, 4)].reshape(4 * HD, length),
            dp[...],
            (((1,), (1,)), ((), ())),
            preferred_element_type=F32,
        ).astype(BF16)
        for j in range(4):
            block = part[j * HD : (j + 1) * HD]
            owner = 4 * j + g
            g_own[owner, 0:HD, :] = block[:, 0:128]
            g_own[owner, HD : HD + HD // 2, :] = jnp.concatenate(
                [block[0 : HD // 2, 128:], block[HD // 2 :, 128:]], axis=1
            )

            @pl.when(owner != d)
            def _():
                rem_copy(
                    g_own.at[owner], g_got.at[d], g1_s.at[owner], g1_r.at[d], {"dp": owner, "tm": t}
                ).start()

    g_got[d] = g_own[d]
    t_got[d] = t_own[...].astype(BF16)
    for i in range(1, N):
        peer = lax.rem(d + i, N)
        copy = rem_copy(t_got.at[d], t_got.at[d], t1_s.at[i], t1_r.at[i], {"dp": peer, "tm": t})
        copy.start()
        sent.append(copy)

    here = {"dp": d, "tm": t}

    def dp_arrived(buf, slot, send, recv, i):
        ref = buf.at[slot]
        rem_copy(ref, ref, send.at[i], recv.at[i], here).wait_recv()

    for i in range(1, N):
        dp_arrived(o_got, lax.rem(d + N - i, N), o1_s, o1_r, i)
    o_red[...] = jnp.sum(o_got[...].astype(F32), axis=0).astype(BF16)
    for i in range(1, N):
        peer = lax.rem(d + i, N)
        copy = rem_copy(o_red, o_fin.at[d], o2_s.at[i], o2_r.at[i], {"dp": peer, "tm": t})
        copy.start()
        sent.append(copy)
    o_fin[d] = o_red[...]

    for i in range(1, N):
        slot = lax.rem(d + i, N)
        dp_arrived(g_got, slot, g1_s, g1_r, slot)
    g_red[...] = jnp.sum(g_got[...].astype(F32), axis=0).astype(BF16)
    for i in range(1, N):
        peer = lax.rem(d + i, N)
        copy = rem_copy(g_red, g_fin.at[t], g2_s.at[i], g2_r.at[t], {"dp": peer, "tm": d})
        copy.start()
        sent.append(copy)
    last = rem_copy(g_red, g_fin.at[t], g2_s.at[0], g2_r.at[t], {"dp": d, "tm": d})

    @pl.when(t != d)
    def _():
        last.start()

    @pl.when(t == d)
    def _():
        g_fin[t] = g_red[...]

    for i in range(1, N):
        dp_arrived(t_got, lax.rem(d + N - i, N), t1_s, t1_r, i)
        dp_arrived(o_fin, lax.rem(d + N - i, N), o2_s, o2_r, i)
    taps_out[...] = jnp.sum(t_got[...].astype(F32), axis=0)
    for j in range(4):
        out_out[:, j * 4 * HD : (j + 1) * 4 * HD] = jnp.concatenate(
            [o_fin[4 * j + k] for k in range(4)], axis=1
        )

    for i in range(1, N):
        slot = lax.rem(t + i, N)
        dp_arrived(g_fin, slot, g2_s, g2_r, slot)

    @pl.when(t != d)
    def _():
        dp_arrived(g_fin, t, g2_s, g2_r, t)
        last.wait_send()

    for j in range(4):
        first, second = [], []
        for k in range(4):
            s = 4 * j + k
            wide = g_fin[s, 0:HD, :]
            tail = g_fin[s, HD : HD + HD // 2, :]
            first.append(wide[:, 0:HD])
            second.append(wide[:, HD:])
            second.append(jnp.concatenate([tail[:, 0:64], tail[:, 64:]], axis=0))
        cols = slice(j * 4 * HD, (j + 1) * 4 * HD)
        glu_out[:, cols] = jnp.concatenate(first, axis=1)
        cols = slice(width + j * 4 * HD, width + (j + 1) * 4 * HD)
        glu_out[:, cols] = jnp.concatenate(second, axis=1)

    for copy in sent:
        copy.wait_send()
    for i in range(1, N):
        owner = lax.rem(d + i, N)
        rem_copy(g_own.at[owner], g_got.at[d], g1_s.at[owner], g1_r.at[d], here).wait_send()
    cot.sent()
    ug.sent()


def vmem():
    return pl.BlockSpec(memory_space=pltpu.VMEM)


def core(query, keys, values, frames, w_glu, w_out, cot, taps, norm_gain, conv_gain):
    rows, width = query.shape
    length = rows * N
    kernel = taps.shape[0]
    lanes = 128
    packed = HD + HD // 2
    dma = pltpu.SemaphoreType.DMA
    V = pltpu.VMEM
    return pl.pallas_call(
        core_kernel,
        out_shape=(
            jax.ShapeDtypeStruct((HD, 2 * width), BF16),
            jax.ShapeDtypeStruct((HD, width), BF16),
            jax.ShapeDtypeStruct((kernel, lanes), F32),
        ),
        in_specs=[vmem()] * 10,
        out_specs=(vmem(), vmem(), vmem()),
        scratch_shapes=[
            V((N, 2 * HD, rows), BF16),
            V((N, 2 * HD, rows), BF16),
            V((N, 2 * HD, rows), BF16),
            V((N, 2 * HD, rows), BF16),
            V((length, HD), BF16),
            V((HD, length), BF16),
            V((HD, length), F32),
            V((N, 2, length), F32),
            V((N, 2, length), F32),
            V((N, 2, length), F32),
            V((N, HD, 2 * HD), BF16),
            V((N, HD, 2 * HD), BF16),
            V((N, HD, length), BF16),
            V((N, rows, width), BF16),
            V((width, 128), F32),
            V((kernel, lanes), F32),
            V((2 * HD, length), F32),
            V((HD, length), F32),
            V((length + kernel, lanes), F32),
            V((length + kernel, lanes), F32),
            V((HD, length), F32),
            V((HD, length), F32),
            V((HD, length), BF16),
            V((2 * HD, length), BF16),
            V((kernel, lanes), F32),
            V((N, packed, 128), BF16),
            V((N, HD, HD), BF16),
            V((N, packed, 128), BF16),
            V((N, HD, HD), BF16),
            V((N, kernel, lanes), BF16),
            V((packed, 128), BF16),
            V((HD, HD), BF16),
            V((N, packed, 128), BF16),
            V((N, HD, HD), BF16),
        ]
        + [dma((N,))] * 12
        + [dma((15,))] * 4
        + [dma((N,))] * 10
        + [dma(())],
        compiler_params=pltpu.CompilerParams(
            collective_id=0, has_side_effects=True, vmem_limit_bytes=58 * 2**20
        ),
        name="core",
    )(query, keys, values, frames, w_glu, w_out, cot, taps, norm_gain, conv_gain)


def local(frames, query, keys, values, norm_gain, conv_gain, w_glu, taps, w_out, cotangent):
    glu_grad, out_grad, taps_grad = core(
        query[0], keys[0], values[0], frames[0], w_glu, w_out, cotangent[0], taps,
        norm_gain.reshape(1, -1), conv_gain.reshape(1, -1),
    )
    return glu_grad.astype(F32), taps_grad[:, :HD], out_grad.astype(F32)


def solution(mesh):
    return jax.shard_map(
        local,
        mesh=mesh,
        in_specs=(
            P("dp", "tm", None),
            P("dp", "tm", None),
            P("dp", "tm", None),
            P("dp", "tm", None),
            P(),
            P(),
            P("tm", None),
            P(),
            P("tm", None),
            P("dp", "tm", None),
        ),
        out_specs=(P("tm", None), P(None, "tm"), P("tm", None)),
        check_vma=False,
    )
```

```python
import functools

import jax
import jax.numpy as jnp
from jax import lax
from jax.experimental import pallas as pl
from jax.experimental.pallas import tpu as pltpu
from jax.sharding import PartitionSpec as P

N = 16
HD = 96
MESH = pl.DeviceIdType.MESH
F32 = jnp.float32
BF16 = jnp.bfloat16
EPS = 1e-05


def rem_copy(src, dst, send, recv, peer):
    return pltpu.make_async_remote_copy(
        src_ref=src, dst_ref=dst, send_sem=send, recv_sem=recv, device_id=peer, device_id_type=MESH
    )


class Gather:
    def __init__(self, me, own, out, slot, send, recv):
        self.own, self.out, self.slot, self.send, self.recv = own, out, slot, send, recv
        y = me // 4
        z = lax.rem(me // 2, 2)
        c = lax.rem(me, 2)
        at = lambda yy, zz, cc: lax.rem(yy, 4) * 4 + zz * 2 + cc
        self.me = me
        self.far = at(y, 1 - z, c)
        self.sib = at(y, z, 1 - c)
        self.to = [at(y + j, z, c) for j in range(1, 4)]
        self.frm = [at(y + 4 - j, z, c) for j in range(1, 4)]
        self.frm_far = [at(y + 4 - j, 1 - z, c) for j in range(1, 4)]
        self.frm_sib = (
            [self.sib, at(y, 1 - z, 1 - c)]
            + [at(y + 4 - j, z, 1 - c) for j in range(1, 4)]
            + [at(y + 4 - j, 1 - z, 1 - c) for j in range(1, 4)]
        )
        self.started = []

    def go(self, src, block, sem, peer):
        copy = rem_copy(
            src, self.out.at[self.slot(block)], self.send.at[sem], self.recv.at[sem], {"tm": peer}
        )
        copy.start()
        self.started.append(copy)

    def on(self, block, sem, peer):
        self.go(self.out.at[self.slot(block)], block, sem, peer)

    def landed(self, block, sem):
        ref = self.out.at[self.slot(block)]
        rem_copy(ref, ref, self.send.at[sem], self.recv.at[sem], {"tm": self.sib}).wait_recv()

    def start_far(self):
        self.go(self.own, self.me, 0, self.far)

    def start_near(self):
        for j in (0, 2, 1):
            self.go(self.own, self.me, 1 + j, self.to[j])
        self.go(self.own, self.me, 7, self.sib)

    def start(self):
        self.start_far()
        self.start_near()

    def relay_far(self):
        self.landed(self.far, 0)
        for j in (0, 2, 1):
            self.on(self.far, 4 + j, self.to[j])
        self.on(self.far, 8, self.sib)

    def relay_near(self):
        for j in (0, 2, 1):
            self.landed(self.frm[j], 1 + j)
            self.on(self.frm[j], 9 + j, self.sib)

    def relay_rest(self):
        for j in (0, 2, 1):
            self.landed(self.frm_far[j], 4 + j)
            self.on(self.frm_far[j], 12 + j, self.sib)

    def near_from_sibling(self):
        for k in (0, 2, 3, 4):
            self.landed(self.frm_sib[k], 7 + k)

    def rest_from_sibling(self):
        for k in (1, 5, 6, 7):
            self.landed(self.frm_sib[k], 7 + k)

    def sent(self):
        for copy in self.started:
            copy.wait_send()


class Swap:
    def __init__(self, me, buf, send, recv):
        self.me, self.buf, self.send, self.recv = me, buf, send, recv
        self.started = []

    def start(self):
        for i in range(1, N):
            copy = rem_copy(
                self.buf.at[self.me],
                self.buf.at[self.me],
                self.send.at[i],
                self.recv.at[i],
                {"tm": lax.rem(self.me + i, N)},
            )
            copy.start()
            self.started.append(copy)

    def finish(self):
        for i in range(1, N):
            ref = self.buf.at[lax.rem(self.me + N - i, N)]
            rem_copy(ref, ref, self.send.at[i], self.recv.at[i], {"tm": self.me}).wait_recv()
        for copy in self.started:
            copy.wait_send()


def own_stats(x):
    mean = jnp.mean(x, axis=0, keepdims=True)
    dev = x - mean
    return mean, jnp.sum(dev * dev, axis=0, keepdims=True)


def joined_stats(buf):
    means = buf[:, 0, :]
    squares = buf[:, 1, :]
    mean = jnp.mean(means, axis=0, keepdims=True)
    dev = means - mean
    total = jnp.sum(squares, axis=0, keepdims=True) + HD * jnp.sum(dev * dev, axis=0, keepdims=True)
    return mean, lax.rsqrt(total * (1.0 / (N * HD)) + EPS)


def core_kernel(
    q_ref, k_ref, v_ref, f_ref, wg_ref, wo_ref, cot_ref, taps_ref, ng_ref, cg_ref,
    glu_out, out_out, taps_out,
    kv_own, qf_own, kv, qf, k_rows, v_cols, mixed, stats, stats_z, stats_e,
    w_own, w_got, u_all, cot_all, small, taps_own, p, ds, y_pad, dz_pad, z_cols, g_cols, s_cols, dp,
    t_own, g_own, o_own, g_got, o_got, t_got, g_red, o_red, g_fin, o_fin,
    kv_s, kv_r, qf_s, qf_r, w_s, w_r, st_s, st_r, sz_s, sz_r, se_s, se_r,
    c_s, c_r, u_s, u_r, g1_s, g1_r, o1_s, o1_r, t1_s, t1_r, g2_s, g2_r, o2_s, o2_r, wx_s, wx_r, own_sem,
):
    d = lax.axis_index("dp")
    t = lax.axis_index("tm")
    rows = q_ref.shape[0]
    length = mixed.shape[1]
    kernel = taps_ref.shape[0]
    half = kernel // 2
    y_at = t // 4
    group = lax.rem(t, 4)
    place = lambda block: lax.rem(block, 4) * 4 + block // 4

    barrier = pltpu.get_barrier_semaphore()

    def greet(dp_at, tm_at):
        pl.semaphore_signal(
            barrier, inc=1, device_id={"dp": dp_at, "tm": tm_at}, device_id_type=MESH
        )

    for i in range(1, N):
        greet(d, lax.rem(t + i, N))
        greet(lax.rem(d + i, N), t)
        greet(lax.rem(d + i, N), d)
        greet(t, lax.rem(t + i, N))

    @pl.when(t != d)
    def _():
        greet(d, d)
        greet(t, t)

    def turn_into(ref, buf, a):
        turned = jnp.transpose(ref[...])
        for j in range(N):
            buf[j, a * HD : (a + 1) * HD, :] = turned[j * HD : (j + 1) * HD]

    sent = []

    def scatter(src, dst, slot, send, recv):
        for i in range(1, N):
            peer = lax.rem(t + i, N)
            copy = rem_copy(src.at[peer], dst.at[slot], send.at[i], recv.at[i], {"tm": peer})
            copy.start()
            sent.append(copy)

    def arrived(dst, slot, i, send, recv):
        ref = dst.at[slot]
        rem_copy(ref, ref, send.at[i], recv.at[i], {"tm": t}).wait_recv()

    turn_into(k_ref, kv_own, 0)
    turn_into(v_ref, kv_own, 1)
    cot_keep = pltpu.make_async_copy(cot_ref, cot_all.at[t], own_sem)
    cot_keep.start()
    pl.semaphore_wait(barrier, jnp.where(t == d, 4 * (N - 1), 4 * (N - 1) + 2))
    scatter(kv_own, kv, t, kv_s, kv_r)
    turn_into(q_ref, qf_own, 0)
    turn_into(f_ref, qf_own, 1)
    scatter(qf_own, qf, t, qf_s, qf_r)
    cot = Gather(t, cot_ref, cot_all, lambda block: block, c_s, c_r)
    cot.start_near()
    width = N * HD
    for j in range(N):
        w_own[j] = jnp.concatenate(
            [
                wg_ref[:, j * HD : (j + 1) * HD],
                wg_ref[:, width + j * HD : width + (j + 1) * HD],
            ],
            axis=1,
        )
    x_at = d // 4
    for i in range(1, N):
        peer = lax.rem(t + i, N)

        @pl.when(x_at == y_at)
        def _():
            rem_copy(
                w_own.at[peer], w_got.at[y_at, group], w_s.at[i], w_r.at[group], {"tm": peer}
            ).start()

    kv[t] = kv_own[t]
    qf[t] = qf_own[t]

    @pl.when(x_at == y_at)
    def _():
        w_got[y_at, group] = w_own[t]


    small[...] = jnp.transpose(
        jnp.concatenate(
            [
                taps_ref[...],
                ng_ref[...].reshape(1, width),
                cg_ref[...].reshape(1, width),
                jnp.zeros((128 - kernel - 2, width), F32),
            ],
            axis=0,
        )
    )
    mine = small[pl.ds(pl.multiple_of(t * HD, HD), HD), :]
    lanes = taps_own.shape[1]
    blank = jnp.zeros((lanes - HD, 128), F32)
    taps_own[...] = jnp.transpose(jnp.concatenate([mine, blank], axis=0))[0:kernel]
    norm_gain = mine[:, kernel : kernel + 1]
    conv_gain = mine[:, kernel + 1 : kernel + 2]
    edge = jnp.zeros((half, lanes), F32)
    for pad in (y_pad, dz_pad):
        pad[0:half, :] = edge
        pad[length + half : length + 2 * half, :] = edge

    for i in range(1, N):
        arrived(kv, lax.rem(t + N - i, N), i, kv_s, kv_r)
    for s in range(N):
        k_rows[s * rows : (s + 1) * rows, :] = jnp.transpose(kv[s, 0:HD, :])
        v_cols[:, s * rows : (s + 1) * rows] = kv[s, HD : 2 * HD, :]
    cot.start_far()

    factor = HD ** -0.5 * 1.4426950408889634
    pair = 2

    @pl.loop(0, N // pair)
    def attend(i):
        for j in range(pair):
            s = i * pair + j

            @pl.when(s != t)
            def _():
                arrived(qf, s, lax.rem(t + N - s, N), qf_s, qf_r)

        queries = jnp.concatenate([qf[i * pair + j, 0:HD, :] for j in range(pair)], axis=1)
        field = jnp.concatenate([qf[i * pair + j, HD : 2 * HD, :] for j in range(pair)], axis=1)
        scores = jnp.dot(k_rows[...], queries, preferred_element_type=F32)
        top = jnp.max(scores, axis=0, keepdims=True)
        expo = jnp.exp2(scores * factor - top * factor)
        total = jnp.sum(expo, axis=0, keepdims=True)
        summed = jnp.dot(v_cols[...], expo.astype(BF16), preferred_element_type=F32)
        attention = (summed / total).astype(BF16)
        block = field.astype(F32) + attention.astype(F32)
        cols = pl.ds(pl.multiple_of(i * pair * rows, pair * rows), pair * rows)
        mixed[:, cols] = block
        mean, square = own_stats(block)
        stats[t, 0:1, cols] = mean
        stats[t, 1:2, cols] = square

    swap = Swap(t, stats, st_s, st_r)
    swap.start()
    for g in range(4):

        @pl.when(x_at * 4 + g != t)
        def _():
            ref = w_got.at[x_at, g]
            rem_copy(ref, ref, w_s.at[0], w_r.at[g], {"tm": t}).wait_recv()

    for i in range(1, 4):
        ref = w_got.at[x_at]
        copy = rem_copy(
            ref, ref, wx_s.at[i], wx_r.at[i], {"dp": lax.rem(d + 4 * i, N), "tm": t}
        )
        copy.start()
        sent.append(copy)
    cot.relay_near()
    swap.finish()
    mean, inv = joined_stats(stats)
    u_all[place(t)] = ((mixed[...] - mean) * inv * norm_gain).astype(BF16)
    ug = Gather(t, u_all.at[place(t)], u_all, place, u_s, u_r)
    ug.start()

    def back_rows(z):
        @pl.loop(0, 4)
        def _(yy):
            first = yy * 4 + z * 2
            block = cot_all[pl.ds(first, 2)].reshape(2 * rows, width)
            ds[:, pl.ds(pl.multiple_of(first * rows, 2 * rows), 2 * rows)] = lax.dot_general(
                wo_ref[...], block, (((1,), (1,)), ((), ())), preferred_element_type=F32
            )

    z_at = lax.rem(t // 2, 2)
    cot.near_from_sibling()
    cot_keep.wait()
    back_rows(z_at)

    for i in range(1, 4):
        ref = w_got.at[lax.rem(x_at + 4 - i, 4)]
        rem_copy(ref, ref, wx_s.at[i], wx_r.at[i], {"tm": t}).wait_recv()
    chunk = 512

    def product(g, first):
        weights = w_got[:, pl.ds(g, 1)].reshape(4 * HD, 2 * HD)

        @pl.loop(0, length // chunk)
        def _(i):
            cols = pl.ds(pl.multiple_of(i * chunk, chunk), chunk)
            part = u_all[pl.ds(g * 4, 4), :, cols].reshape(4 * HD, chunk)
            part = lax.dot_general(
                weights, part, (((0,), (0,)), ((), ())), preferred_element_type=F32
            )
            p[:, cols] = part if first else p[:, cols] + part

    side = lax.rem(group + 1, 2) - lax.rem(group, 2)
    ug.relay_far()
    ug.relay_near()
    product(group, True)
    ug.near_from_sibling()
    product(group + side, False)
    ug.relay_rest()
    cot.relay_far()
    other = lax.rem(group + 2, 4)
    product(other, False)
    ug.rest_from_sibling()
    product(other + side, False)

    step = 128
    blocks = length // step

    @pl.loop(0, blocks)
    def gate(i):
        cols = pl.ds(pl.multiple_of(i * step, step), step)
        y = p[0:HD, cols] * jax.nn.sigmoid(p[HD : 2 * HD, cols])
        y = y.astype(BF16).astype(F32)
        y_pad[pl.ds(pl.multiple_of(half + i * step, half), step), :] = jnp.transpose(
            jnp.concatenate([y, blank], axis=0)
        )

    @pl.loop(0, blocks)
    def conv(i):
        start = pl.multiple_of(i * step, step)
        z = jnp.zeros((step, lanes), F32)
        for k in range(kernel):
            z = z + taps_own[k : k + 1, :] * y_pad[pl.ds(start + k, step), :]
        z = jnp.transpose(z)[0:HD]
        cols = pl.ds(start, step)
        z_cols[:, cols] = z
        mean, square = own_stats(z)
        stats_z[t, 0:1, cols] = mean
        stats_z[t, 1:2, cols] = square

    swap = Swap(t, stats_z, sz_s, sz_r)
    swap.start()
    cot.relay_rest()
    cot.rest_from_sibling()
    back_rows(1 - z_at)
    swap.finish()
    mean, inv = joined_stats(stats_z)
    zhat = (z_cols[...] - mean) * inv
    z_cols[...] = zhat
    n = zhat * conv_gain
    sgate = jax.nn.sigmoid(n)
    s_cols[...] = (n * sgate).astype(BF16)
    e = ds[...] * sgate * (1.0 + n * (1.0 - sgate)) * conv_gain
    g_cols[...] = e
    stats_e[t, 0:1, :] = jnp.sum(e, axis=0, keepdims=True)
    stats_e[t, 1:2, :] = jnp.sum(e * zhat, axis=0, keepdims=True)
    swap_e = Swap(t, stats_e, se_s, se_r)
    swap_e.start()

    for j in range(4):
        cols = slice(j * 4 * HD, (j + 1) * 4 * HD)
        part = jnp.dot(
            s_cols[...], cot_all[:, :, cols].reshape(length, 4 * HD), preferred_element_type=F32
        ).astype(BF16)
        for k in range(4):
            o_own[4 * j + k] = part[:, k * HD : (k + 1) * HD]
    for i in range(1, N):
        peer = lax.rem(d + i, N)
        copy = rem_copy(o_own.at[peer], o_got.at[d], o1_s.at[i], o1_r.at[i], {"dp": peer, "tm": t})
        copy.start()
        sent.append(copy)
    o_got[d] = o_own[d]

    swap_e.finish()
    sums = jnp.sum(stats_e[...], axis=0) * (1.0 / (N * HD))
    g_cols[...] = (
        ((g_cols[...] - sums[0:1] - z_cols[...] * sums[1:2]) * inv).astype(BF16).astype(F32)
    )

    @pl.loop(0, blocks)
    def turn(i):
        cols = pl.ds(pl.multiple_of(i * step, step), step)
        dz_pad[pl.ds(pl.multiple_of(half + i * step, half), step), :] = jnp.transpose(
            jnp.concatenate([g_cols[:, cols], blank], axis=0)
        )

    @pl.loop(0, blocks)
    def back(i):
        start = pl.multiple_of(i * step, step)
        dy = jnp.zeros((step, lanes), F32)
        for k in range(kernel):
            dy = dy + taps_own[k : k + 1, :] * dz_pad[pl.ds(start + 2 * half - k, step), :]
        dy = jnp.transpose(dy)[0:HD]
        cols = pl.ds(start, step)
        pa = p[0:HD, cols]
        sig = jax.nn.sigmoid(p[HD : 2 * HD, cols])
        dp[0:HD, cols] = (dy * sig).astype(BF16)
        dp[HD : 2 * HD, cols] = (dy * pa * sig * (1.0 - sig)).astype(BF16)

    @pl.loop(0, 4)
    def grads(i):
        g = lax.rem(i + d, 4)
        part = lax.dot_general(
            u_all[pl.ds(g * 4, 4)].reshape(4 * HD, length),
            dp[...],
            (((1,), (1,)), ((), ())),
            preferred_element_type=F32,
        ).astype(BF16)
        for j in range(4):
            block = part[j * HD : (j + 1) * HD]
            owner = 4 * j + g
            g_own[owner, 0:HD, :] = block[:, 0:128]
            g_own[owner, HD : HD + HD // 2, :] = jnp.concatenate(
                [block[0 : HD // 2, 128:], block[HD // 2 :, 128:]], axis=1
            )

            @pl.when(owner != d)
            def _():
                rem_copy(
                    g_own.at[owner], g_got.at[d], g1_s.at[owner], g1_r.at[d], {"dp": owner, "tm": t}
                ).start()

    g_got[d] = g_own[d]
    t_own[...] = jnp.zeros_like(t_own)

    @pl.loop(0, blocks)
    def tap_grads(i):
        start = pl.multiple_of(i * step, step)
        dz = dz_pad[pl.ds(pl.multiple_of(half + start, half), step), :]
        for k in range(kernel):
            prod = dz * y_pad[pl.ds(start + k, step), :]
            t_own[k : k + 1, :] += jnp.sum(prod, axis=0, keepdims=True)

    t_got[d] = t_own[...].astype(BF16)
    for i in range(1, N):
        peer = lax.rem(d + i, N)
        copy = rem_copy(t_got.at[d], t_got.at[d], t1_s.at[i], t1_r.at[i], {"dp": peer, "tm": t})
        copy.start()
        sent.append(copy)

    here = {"dp": d, "tm": t}

    def dp_arrived(buf, slot, send, recv, i):
        ref = buf.at[slot]
        rem_copy(ref, ref, send.at[i], recv.at[i], here).wait_recv()

    for i in range(1, N):
        dp_arrived(o_got, lax.rem(d + N - i, N), o1_s, o1_r, i)
    o_red[...] = jnp.sum(o_got[...].astype(F32), axis=0).astype(BF16)
    for i in range(1, N):
        peer = lax.rem(d + i, N)
        copy = rem_copy(o_red, o_fin.at[d], o2_s.at[i], o2_r.at[i], {"dp": peer, "tm": t})
        copy.start()
        sent.append(copy)
    o_fin[d] = o_red[...]

    for i in range(1, N):
        slot = lax.rem(d + i, N)
        dp_arrived(g_got, slot, g1_s, g1_r, slot)
    g_red[...] = jnp.sum(g_got[...].astype(F32), axis=0).astype(BF16)
    for i in range(1, N):
        peer = lax.rem(d + i, N)
        copy = rem_copy(g_red, g_fin.at[t], g2_s.at[i], g2_r.at[t], {"dp": peer, "tm": d})
        copy.start()
        sent.append(copy)
    last = rem_copy(g_red, g_fin.at[t], g2_s.at[0], g2_r.at[t], {"dp": d, "tm": d})

    @pl.when(t != d)
    def _():
        last.start()

    @pl.when(t == d)
    def _():
        g_fin[t] = g_red[...]

    for i in range(1, N):
        dp_arrived(t_got, lax.rem(d + N - i, N), t1_s, t1_r, i)
        dp_arrived(o_fin, lax.rem(d + N - i, N), o2_s, o2_r, i)
    taps_out[...] = jnp.sum(t_got[...].astype(F32), axis=0)
    for j in range(4):
        out_out[:, j * 4 * HD : (j + 1) * 4 * HD] = jnp.concatenate(
            [o_fin[4 * j + k] for k in range(4)], axis=1
        )

    for i in range(1, N):
        slot = lax.rem(t + i, N)
        dp_arrived(g_fin, slot, g2_s, g2_r, slot)

    @pl.when(t != d)
    def _():
        dp_arrived(g_fin, t, g2_s, g2_r, t)
        last.wait_send()

    for j in range(4):
        first, second = [], []
        for k in range(4):
            s = 4 * j + k
            wide = g_fin[s, 0:HD, :]
            tail = g_fin[s, HD : HD + HD // 2, :]
            first.append(wide[:, 0:HD])
            second.append(wide[:, HD:])
            second.append(jnp.concatenate([tail[:, 0:64], tail[:, 64:]], axis=0))
        cols = slice(j * 4 * HD, (j + 1) * 4 * HD)
        glu_out[:, cols] = jnp.concatenate(first, axis=1)
        cols = slice(width + j * 4 * HD, width + (j + 1) * 4 * HD)
        glu_out[:, cols] = jnp.concatenate(second, axis=1)

    for copy in sent:
        copy.wait_send()
    for i in range(1, N):

        @pl.when(x_at == y_at)
        def _():
            ref = w_own.at[lax.rem(t + i, N)]
            rem_copy(ref, ref, w_s.at[i], w_r.at[group], {"tm": t}).wait_send()

    for i in range(1, N):
        owner = lax.rem(d + i, N)
        rem_copy(g_own.at[owner], g_got.at[d], g1_s.at[owner], g1_r.at[d], here).wait_send()
    cot.sent()
    ug.sent()


def vmem():
    return pl.BlockSpec(memory_space=pltpu.VMEM)


def core(query, keys, values, frames, w_glu, w_out, cot, taps, norm_gain, conv_gain):
    rows, width = query.shape
    length = rows * N
    kernel = taps.shape[0]
    lanes = 128
    packed = HD + HD // 2
    dma = pltpu.SemaphoreType.DMA
    V = pltpu.VMEM
    return pl.pallas_call(
        core_kernel,
        out_shape=(
            jax.ShapeDtypeStruct((HD, 2 * width), BF16),
            jax.ShapeDtypeStruct((HD, width), BF16),
            jax.ShapeDtypeStruct((kernel, lanes), F32),
        ),
        in_specs=[vmem()] * 10,
        out_specs=(vmem(), vmem(), vmem()),
        scratch_shapes=[
            V((N, 2 * HD, rows), BF16),
            V((N, 2 * HD, rows), BF16),
            V((N, 2 * HD, rows), BF16),
            V((N, 2 * HD, rows), BF16),
            V((length, HD), BF16),
            V((HD, length), BF16),
            V((HD, length), F32),
            V((N, 2, length), F32),
            V((N, 2, length), F32),
            V((N, 2, length), F32),
            V((N, HD, 2 * HD), BF16),
            V((4, 4, HD, 2 * HD), BF16),
            V((N, HD, length), BF16),
            V((N, rows, width), BF16),
            V((width, 128), F32),
            V((kernel, lanes), F32),
            V((2 * HD, length), F32),
            V((HD, length), F32),
            V((length + kernel, lanes), F32),
            V((length + kernel, lanes), F32),
            V((HD, length), F32),
            V((HD, length), F32),
            V((HD, length), BF16),
            V((2 * HD, length), BF16),
            V((kernel, lanes), F32),
            V((N, packed, 128), BF16),
            V((N, HD, HD), BF16),
            V((N, packed, 128), BF16),
            V((N, HD, HD), BF16),
            V((N, kernel, lanes), BF16),
            V((packed, 128), BF16),
            V((HD, HD), BF16),
            V((N, packed, 128), BF16),
            V((N, HD, HD), BF16),
        ]
        + [dma((N,))] * 12
        + [dma((15,))] * 4
        + [dma((N,))] * 10
        + [dma((4,))] * 2
        + [dma(())],
        compiler_params=pltpu.CompilerParams(
            collective_id=0, has_side_effects=True, vmem_limit_bytes=58 * 2**20
        ),
        name="core",
    )(query, keys, values, frames, w_glu, w_out, cot, taps, norm_gain, conv_gain)


def local(frames, query, keys, values, norm_gain, conv_gain, w_glu, taps, w_out, cotangent):
    glu_grad, out_grad, taps_grad = core(
        query[0], keys[0], values[0], frames[0], w_glu, w_out, cotangent[0], taps,
        norm_gain, conv_gain,
    )
    return glu_grad.astype(F32), taps_grad[:, :HD], out_grad.astype(F32)


def solution(mesh):
    return jax.shard_map(
        local,
        mesh=mesh,
        in_specs=(
            P("dp", "tm", None),
            P("dp", "tm", None),
            P("dp", "tm", None),
            P("dp", "tm", None),
            P(),
            P(),
            P("tm", None),
            P(),
            P("tm", None),
            P("dp", "tm", None),
        ),
        out_specs=(P("tm", None), P(None, "tm"), P("tm", None)),
        check_vma=False,
    )
```

```python
import functools

import jax
import jax.numpy as jnp
from jax import lax
from jax.experimental import pallas as pl
from jax.experimental.pallas import tpu as pltpu
from jax.sharding import PartitionSpec as P

N = 16
HD = 96
MESH = pl.DeviceIdType.MESH
F32 = jnp.float32
BF16 = jnp.bfloat16
EPS = 1e-05


def rem_copy(src, dst, send, recv, peer):
    return pltpu.make_async_remote_copy(
        src_ref=src, dst_ref=dst, send_sem=send, recv_sem=recv, device_id=peer, device_id_type=MESH
    )


class Gather:
    def __init__(self, me, own, out, slot, send, recv):
        self.own, self.out, self.slot, self.send, self.recv = own, out, slot, send, recv
        y = me // 4
        z = lax.rem(me // 2, 2)
        c = lax.rem(me, 2)
        at = lambda yy, zz, cc: lax.rem(yy, 4) * 4 + zz * 2 + cc
        self.me = me
        self.far = at(y, 1 - z, c)
        self.sib = at(y, z, 1 - c)
        self.to = [at(y + j, z, c) for j in range(1, 4)]
        self.frm = [at(y + 4 - j, z, c) for j in range(1, 4)]
        self.frm_far = [at(y + 4 - j, 1 - z, c) for j in range(1, 4)]
        self.frm_sib = (
            [self.sib, at(y, 1 - z, 1 - c)]
            + [at(y + 4 - j, z, 1 - c) for j in range(1, 4)]
            + [at(y + 4 - j, 1 - z, 1 - c) for j in range(1, 4)]
        )
        self.started = []

    def go(self, src, block, sem, peer):
        copy = rem_copy(
            src, self.out.at[self.slot(block)], self.send.at[sem], self.recv.at[sem], {"tm": peer}
        )
        copy.start()
        self.started.append(copy)

    def on(self, block, sem, peer):
        self.go(self.out.at[self.slot(block)], block, sem, peer)

    def landed(self, block, sem):
        ref = self.out.at[self.slot(block)]
        rem_copy(ref, ref, self.send.at[sem], self.recv.at[sem], {"tm": self.sib}).wait_recv()

    def start_far(self):
        self.go(self.own, self.me, 0, self.far)

    def start_near(self):
        for j in (0, 2, 1):
            self.go(self.own, self.me, 1 + j, self.to[j])
        self.go(self.own, self.me, 7, self.sib)

    def start(self):
        self.start_far()
        self.start_near()

    def relay_far(self):
        self.landed(self.far, 0)
        for j in (0, 2, 1):
            self.on(self.far, 4 + j, self.to[j])
        self.on(self.far, 8, self.sib)

    def relay_near(self):
        for j in (0, 2, 1):
            self.landed(self.frm[j], 1 + j)
            self.on(self.frm[j], 9 + j, self.sib)

    def relay_rest(self):
        for j in (0, 2, 1):
            self.landed(self.frm_far[j], 4 + j)
            self.on(self.frm_far[j], 12 + j, self.sib)

    def near_from_sibling(self):
        for k in (0, 2, 3, 4):
            self.landed(self.frm_sib[k], 7 + k)

    def rest_from_sibling(self):
        for k in (1, 5, 6, 7):
            self.landed(self.frm_sib[k], 7 + k)

    def sent(self):
        for copy in self.started:
            copy.wait_send()


class Swap:
    def __init__(self, me, buf, send, recv):
        self.me, self.buf, self.send, self.recv = me, buf, send, recv
        self.started = []

    def start(self):
        for i in range(1, N):
            copy = rem_copy(
                self.buf.at[self.me],
                self.buf.at[self.me],
                self.send.at[i],
                self.recv.at[i],
                {"tm": lax.rem(self.me + i, N)},
            )
            copy.start()
            self.started.append(copy)

    def finish(self):
        for i in range(1, N):
            ref = self.buf.at[lax.rem(self.me + N - i, N)]
            rem_copy(ref, ref, self.send.at[i], self.recv.at[i], {"tm": self.me}).wait_recv()
        for copy in self.started:
            copy.wait_send()


def own_stats(x):
    mean = jnp.mean(x, axis=0, keepdims=True)
    dev = x - mean
    return mean, jnp.sum(dev * dev, axis=0, keepdims=True)


def joined_stats(buf):
    means = buf[:, 0, :]
    squares = buf[:, 1, :]
    mean = jnp.mean(means, axis=0, keepdims=True)
    dev = means - mean
    total = jnp.sum(squares, axis=0, keepdims=True) + HD * jnp.sum(dev * dev, axis=0, keepdims=True)
    return mean, lax.rsqrt(total * (1.0 / (N * HD)) + EPS)


def core_kernel(
    q_ref, k_ref, v_ref, f_ref, wg_ref, wo_ref, cot_ref, taps_ref, ng_ref, cg_ref,
    glu_out, out_out, taps_out,
    kv_own, qf_own, kv, qf, k_rows, v_cols, mixed, stats_a, stats_b, stats_z, stats_e,
    w_own, w_got, u_all, cot_all, small, taps_own, p, ds, y_pad, dz_pad, z_cols, g_cols, s_cols, dp,
    t_own, g_own, o_own, g_got, o_got, t_got, g_red, o_red, g_fin, o_fin,
    kv_s, kv_r, qf_s, qf_r, w_s, w_r, st_s, st_r, sz_s, sz_r, se_s, se_r,
    sb_s, sb_r, c_s, c_r, ua_s, ua_r, ub_s, ub_r, g1_s, g1_r, o1_s, o1_r, t1_s, t1_r, g2_s, g2_r, o2_s, o2_r, wx_s, wx_r, own_sem,
):
    d = lax.axis_index("dp")
    t = lax.axis_index("tm")
    rows = q_ref.shape[0]
    length = mixed.shape[1]
    kernel = taps_ref.shape[0]
    half = kernel // 2
    y_at = t // 4
    group = lax.rem(t, 4)
    place = lambda block: lax.rem(block, 4) * 4 + block // 4

    barrier = pltpu.get_barrier_semaphore()

    def greet(dp_at, tm_at):
        pl.semaphore_signal(
            barrier, inc=1, device_id={"dp": dp_at, "tm": tm_at}, device_id_type=MESH
        )

    for i in range(1, N):
        greet(d, lax.rem(t + i, N))
        greet(lax.rem(d + i, N), t)
        greet(lax.rem(d + i, N), d)
        greet(t, lax.rem(t + i, N))

    @pl.when(t != d)
    def _():
        greet(d, d)
        greet(t, t)

    def turn_into(ref, buf, a):
        turned = jnp.transpose(ref[...])
        for j in range(N):
            buf[j, a * HD : (a + 1) * HD, :] = turned[j * HD : (j + 1) * HD]

    sent = []

    def scatter(src, dst, slot, send, recv):
        for i in range(1, N):
            peer = lax.rem(t + i, N)
            copy = rem_copy(src.at[peer], dst.at[slot], send.at[i], recv.at[i], {"tm": peer})
            copy.start()
            sent.append(copy)

    def arrived(dst, slot, i, send, recv):
        ref = dst.at[slot]
        rem_copy(ref, ref, send.at[i], recv.at[i], {"tm": t}).wait_recv()

    turn_into(k_ref, kv_own, 0)
    turn_into(v_ref, kv_own, 1)
    cot_keep = pltpu.make_async_copy(cot_ref, cot_all.at[t], own_sem)
    cot_keep.start()
    pl.semaphore_wait(barrier, jnp.where(t == d, 4 * (N - 1), 4 * (N - 1) + 2))
    scatter(kv_own, kv, t, kv_s, kv_r)
    turn_into(q_ref, qf_own, 0)
    turn_into(f_ref, qf_own, 1)
    scatter(qf_own, qf, t, qf_s, qf_r)
    cot = Gather(t, cot_ref, cot_all, lambda block: block, c_s, c_r)
    cot.start_near()
    width = N * HD
    for j in range(N):
        w_own[j] = jnp.concatenate(
            [
                wg_ref[:, j * HD : (j + 1) * HD],
                wg_ref[:, width + j * HD : width + (j + 1) * HD],
            ],
            axis=1,
        )
    x_at = d // 4
    for i in range(1, N):
        peer = lax.rem(t + i, N)

        @pl.when(x_at == y_at)
        def _():
            rem_copy(
                w_own.at[peer], w_got.at[y_at, group], w_s.at[i], w_r.at[group], {"tm": peer}
            ).start()

    kv[t] = kv_own[t]
    qf[t] = qf_own[t]

    @pl.when(x_at == y_at)
    def _():
        w_got[y_at, group] = w_own[t]


    small[...] = jnp.transpose(
        jnp.concatenate(
            [
                taps_ref[...],
                ng_ref[...].reshape(1, width),
                cg_ref[...].reshape(1, width),
                jnp.zeros((128 - kernel - 2, width), F32),
            ],
            axis=0,
        )
    )
    mine = small[pl.ds(pl.multiple_of(t * HD, HD), HD), :]
    lanes = taps_own.shape[1]
    blank = jnp.zeros((lanes - HD, 128), F32)
    taps_own[...] = jnp.transpose(jnp.concatenate([mine, blank], axis=0))[0:kernel]
    norm_gain = mine[:, kernel : kernel + 1]
    conv_gain = mine[:, kernel + 1 : kernel + 2]
    edge = jnp.zeros((half, lanes), F32)
    for pad in (y_pad, dz_pad):
        pad[0:half, :] = edge
        pad[length + half : length + 2 * half, :] = edge

    for i in range(1, N):
        arrived(kv, lax.rem(t + N - i, N), i, kv_s, kv_r)
    for s in range(N):
        k_rows[s * rows : (s + 1) * rows, :] = jnp.transpose(kv[s, 0:HD, :])
        v_cols[:, s * rows : (s + 1) * rows] = kv[s, HD : 2 * HD, :]
    factor = HD ** -0.5 * 1.4426950408889634
    pair = 2
    middle = length // 2

    def attend(low, high, h, stats):
        @pl.loop(low, high)
        def _(i):
            for j in range(pair):
                s = i * pair + j

                @pl.when(s != t)
                def _():
                    arrived(qf, s, lax.rem(t + N - s, N), qf_s, qf_r)

            queries = jnp.concatenate([qf[i * pair + j, 0:HD, :] for j in range(pair)], axis=1)
            field = jnp.concatenate([qf[i * pair + j, HD : 2 * HD, :] for j in range(pair)], axis=1)
            scores = jnp.dot(k_rows[...], queries, preferred_element_type=F32)
            top = jnp.max(scores, axis=0, keepdims=True)
            expo = jnp.exp2(scores * factor - top * factor)
            total = jnp.sum(expo, axis=0, keepdims=True)
            summed = jnp.dot(v_cols[...], expo.astype(BF16), preferred_element_type=F32)
            attention = (summed / total).astype(BF16)
            block = field.astype(F32) + attention.astype(F32)
            span = pair * rows
            mixed[:, pl.ds(pl.multiple_of(i * span, span), span)] = block
            cols = pl.ds(pl.multiple_of((i - h * (middle // span)) * span, span), span)
            mean, square = own_stats(block)
            stats[t, 0:1, cols] = mean
            stats[t, 1:2, cols] = square

    def make_u(h, stats, send, recv):
        mean, inv = joined_stats(stats)
        v = mixed[:, h * middle : (h + 1) * middle]
        u_all[h, place(t)] = ((v - mean) * inv * norm_gain).astype(BF16)
        gather = Gather(t, u_all.at[h, place(t)], u_all.at[h], place, send, recv)
        gather.start()
        return gather

    attend(0, 4, 0, stats_a)
    swap_a = Swap(t, stats_a, st_s, st_r)
    swap_a.start()
    attend(4, 6, 1, stats_b)
    swap_a.finish()
    ua = make_u(0, stats_a, ua_s, ua_r)
    attend(6, 8, 1, stats_b)
    swap_b = Swap(t, stats_b, sb_s, sb_r)
    swap_b.start()
    for g in range(4):

        @pl.when(x_at * 4 + g != t)
        def _():
            ref = w_got.at[x_at, g]
            rem_copy(ref, ref, w_s.at[0], w_r.at[g], {"tm": t}).wait_recv()

    for i in range(1, 4):
        ref = w_got.at[x_at]
        copy = rem_copy(
            ref, ref, wx_s.at[i], wx_r.at[i], {"dp": lax.rem(d + 4 * i, N), "tm": t}
        )
        copy.start()
        sent.append(copy)
    swap_b.finish()
    ub = make_u(1, stats_b, ub_s, ub_r)
    ua.relay_far()
    ua.relay_near()
    cot.start_far()
    cot.relay_near()

    def back_rows(z):
        @pl.loop(0, 4)
        def _(yy):
            first = yy * 4 + z * 2
            block = cot_all[pl.ds(first, 2)].reshape(2 * rows, width)
            ds[:, pl.ds(pl.multiple_of(first * rows, 2 * rows), 2 * rows)] = lax.dot_general(
                wo_ref[...], block, (((1,), (1,)), ((), ())), preferred_element_type=F32
            )

    z_at = lax.rem(t // 2, 2)
    for i in range(1, 4):
        ref = w_got.at[lax.rem(x_at + 4 - i, 4)]
        rem_copy(ref, ref, wx_s.at[i], wx_r.at[i], {"tm": t}).wait_recv()
    chunk = 512

    def product(g, h, first):
        weights = w_got[:, pl.ds(g, 1)].reshape(4 * HD, 2 * HD)

        @pl.loop(0, middle // chunk)
        def _(i):
            cols = pl.ds(pl.multiple_of(i * chunk, chunk), chunk)
            part = u_all[h, pl.ds(g * 4, 4), :, cols].reshape(4 * HD, chunk)
            part = lax.dot_general(
                weights, part, (((0,), (0,)), ((), ())), preferred_element_type=F32
            )
            cols = pl.ds(pl.multiple_of(h * middle + i * chunk, chunk), chunk)
            p[:, cols] = part if first else p[:, cols] + part

    step = 128
    blocks = length // step

    def gate(low, high):
        @pl.loop(low, high)
        def _(i):
            cols = pl.ds(pl.multiple_of(i * step, step), step)
            y = p[0:HD, cols] * jax.nn.sigmoid(p[HD : 2 * HD, cols])
            y = y.astype(BF16).astype(F32)
            y_pad[pl.ds(pl.multiple_of(half + i * step, half), step), :] = jnp.transpose(
                jnp.concatenate([y, blank], axis=0)
            )

    def conv(low, high):
        @pl.loop(low, high)
        def _(i):
            start = pl.multiple_of(i * step, step)
            z = jnp.zeros((step, lanes), F32)
            for k in range(kernel):
                z = z + taps_own[k : k + 1, :] * y_pad[pl.ds(start + k, step), :]
            z = jnp.transpose(z)[0:HD]
            cols = pl.ds(start, step)
            z_cols[:, cols] = z
            mean, square = own_stats(z)
            stats_z[t, 0:1, cols] = mean
            stats_z[t, 1:2, cols] = square

    side = lax.rem(group + 1, 2) - lax.rem(group, 2)
    other = lax.rem(group + 2, 4)
    product(group, 0, True)
    ua.near_from_sibling()
    product(group + side, 0, False)
    ub.relay_far()
    ub.relay_near()
    ua.relay_rest()
    cot.relay_far()
    cot.near_from_sibling()
    cot_keep.wait()
    back_rows(z_at)
    product(other, 0, False)
    ua.rest_from_sibling()
    product(other + side, 0, False)
    gate(0, blocks // 2)
    product(group, 1, True)
    ub.near_from_sibling()
    product(group + side, 1, False)
    conv(0, blocks // 2 - 1)
    ub.relay_rest()
    product(other, 1, False)
    ub.rest_from_sibling()
    product(other + side, 1, False)
    gate(blocks // 2, blocks)
    conv(blocks // 2 - 1, blocks)

    swap = Swap(t, stats_z, sz_s, sz_r)
    swap.start()
    cot.relay_rest()
    cot.rest_from_sibling()
    back_rows(1 - z_at)
    swap.finish()
    mean, inv = joined_stats(stats_z)
    zhat = (z_cols[...] - mean) * inv
    z_cols[...] = zhat
    n = zhat * conv_gain
    sgate = jax.nn.sigmoid(n)
    s_cols[...] = (n * sgate).astype(BF16)
    e = ds[...] * sgate * (1.0 + n * (1.0 - sgate)) * conv_gain
    g_cols[...] = e
    stats_e[t, 0:1, :] = jnp.sum(e, axis=0, keepdims=True)
    stats_e[t, 1:2, :] = jnp.sum(e * zhat, axis=0, keepdims=True)
    swap_e = Swap(t, stats_e, se_s, se_r)
    swap_e.start()

    for j in range(4):
        cols = slice(j * 4 * HD, (j + 1) * 4 * HD)
        part = jnp.dot(
            s_cols[...], cot_all[:, :, cols].reshape(length, 4 * HD), preferred_element_type=F32
        ).astype(BF16)
        for k in range(4):
            o_own[4 * j + k] = part[:, k * HD : (k + 1) * HD]
    for i in range(1, N):
        peer = lax.rem(d + i, N)
        copy = rem_copy(o_own.at[peer], o_got.at[d], o1_s.at[i], o1_r.at[i], {"dp": peer, "tm": t})
        copy.start()
        sent.append(copy)
    o_got[d] = o_own[d]

    swap_e.finish()
    sums = jnp.sum(stats_e[...], axis=0) * (1.0 / (N * HD))
    g_cols[...] = (
        ((g_cols[...] - sums[0:1] - z_cols[...] * sums[1:2]) * inv).astype(BF16).astype(F32)
    )

    @pl.loop(0, blocks)
    def turn(i):
        cols = pl.ds(pl.multiple_of(i * step, step), step)
        dz_pad[pl.ds(pl.multiple_of(half + i * step, half), step), :] = jnp.transpose(
            jnp.concatenate([g_cols[:, cols], blank], axis=0)
        )

    @pl.loop(0, blocks)
    def back(i):
        start = pl.multiple_of(i * step, step)
        dy = jnp.zeros((step, lanes), F32)
        for k in range(kernel):
            dy = dy + taps_own[k : k + 1, :] * dz_pad[pl.ds(start + 2 * half - k, step), :]
        dy = jnp.transpose(dy)[0:HD]
        cols = pl.ds(start, step)
        pa = p[0:HD, cols]
        sig = jax.nn.sigmoid(p[HD : 2 * HD, cols])
        dp[0:HD, cols] = (dy * sig).astype(BF16)
        dp[HD : 2 * HD, cols] = (dy * pa * sig * (1.0 - sig)).astype(BF16)

    @pl.loop(0, 4)
    def grads(i):
        g = lax.rem(i + d, 4)
        part = [
            lax.dot_general(
                u_all[h, pl.ds(g * 4, 4)].reshape(4 * HD, middle),
                dp[:, h * middle : (h + 1) * middle],
                (((1,), (1,)), ((), ())),
                preferred_element_type=F32,
            )
            for h in range(2)
        ]
        part = (part[0] + part[1]).astype(BF16)
        for j in range(4):
            block = part[j * HD : (j + 1) * HD]
            owner = 4 * j + g
            g_own[owner, 0:HD, :] = block[:, 0:128]
            g_own[owner, HD : HD + HD // 2, :] = jnp.concatenate(
                [block[0 : HD // 2, 128:], block[HD // 2 :, 128:]], axis=1
            )

            @pl.when(owner != d)
            def _():
                rem_copy(
                    g_own.at[owner], g_got.at[d], g1_s.at[owner], g1_r.at[d], {"dp": owner, "tm": t}
                ).start()

    g_got[d] = g_own[d]
    t_own[...] = jnp.zeros_like(t_own)

    @pl.loop(0, blocks)
    def tap_grads(i):
        start = pl.multiple_of(i * step, step)
        dz = dz_pad[pl.ds(pl.multiple_of(half + start, half), step), :]
        for k in range(kernel):
            prod = dz * y_pad[pl.ds(start + k, step), :]
            t_own[k : k + 1, :] += jnp.sum(prod, axis=0, keepdims=True)

    t_got[d] = t_own[...].astype(BF16)
    for i in range(1, N):
        peer = lax.rem(d + i, N)
        copy = rem_copy(t_got.at[d], t_got.at[d], t1_s.at[i], t1_r.at[i], {"dp": peer, "tm": t})
        copy.start()
        sent.append(copy)

    here = {"dp": d, "tm": t}

    def dp_arrived(buf, slot, send, recv, i):
        ref = buf.at[slot]
        rem_copy(ref, ref, send.at[i], recv.at[i], here).wait_recv()

    for i in range(1, N):
        slot = lax.rem(d + i, N)
        dp_arrived(g_got, slot, g1_s, g1_r, slot)
    g_red[...] = jnp.sum(g_got[...].astype(F32), axis=0).astype(BF16)
    for i in range(1, N):
        peer = lax.rem(d + i, N)
        copy = rem_copy(g_red, g_fin.at[t], g2_s.at[i], g2_r.at[t], {"dp": peer, "tm": d})
        copy.start()
        sent.append(copy)
    last = rem_copy(g_red, g_fin.at[t], g2_s.at[0], g2_r.at[t], {"dp": d, "tm": d})

    @pl.when(t != d)
    def _():
        last.start()

    @pl.when(t == d)
    def _():
        g_fin[t] = g_red[...]

    for i in range(1, N):
        dp_arrived(o_got, lax.rem(d + N - i, N), o1_s, o1_r, i)
    o_red[...] = jnp.sum(o_got[...].astype(F32), axis=0).astype(BF16)
    for i in range(1, N):
        peer = lax.rem(d + i, N)
        copy = rem_copy(o_red, o_fin.at[d], o2_s.at[i], o2_r.at[i], {"dp": peer, "tm": t})
        copy.start()
        sent.append(copy)
    o_fin[d] = o_red[...]

    for i in range(1, N):
        dp_arrived(t_got, lax.rem(d + N - i, N), t1_s, t1_r, i)
        dp_arrived(o_fin, lax.rem(d + N - i, N), o2_s, o2_r, i)
    taps_out[...] = jnp.sum(t_got[...].astype(F32), axis=0)
    for j in range(4):
        out_out[:, j * 4 * HD : (j + 1) * 4 * HD] = jnp.concatenate(
            [o_fin[4 * j + k] for k in range(4)], axis=1
        )

    for i in range(1, N):
        slot = lax.rem(t + i, N)
        dp_arrived(g_fin, slot, g2_s, g2_r, slot)

    @pl.when(t != d)
    def _():
        dp_arrived(g_fin, t, g2_s, g2_r, t)
        last.wait_send()

    for j in range(4):
        first, second = [], []
        for k in range(4):
            s = 4 * j + k
            wide = g_fin[s, 0:HD, :]
            tail = g_fin[s, HD : HD + HD // 2, :]
            first.append(wide[:, 0:HD])
            second.append(wide[:, HD:])
            second.append(jnp.concatenate([tail[:, 0:64], tail[:, 64:]], axis=0))
        cols = slice(j * 4 * HD, (j + 1) * 4 * HD)
        glu_out[:, cols] = jnp.concatenate(first, axis=1)
        cols = slice(width + j * 4 * HD, width + (j + 1) * 4 * HD)
        glu_out[:, cols] = jnp.concatenate(second, axis=1)

    for copy in sent:
        copy.wait_send()
    for i in range(1, N):

        @pl.when(x_at == y_at)
        def _():
            ref = w_own.at[lax.rem(t + i, N)]
            rem_copy(ref, ref, w_s.at[i], w_r.at[group], {"tm": t}).wait_send()

    for i in range(1, N):
        owner = lax.rem(d + i, N)
        rem_copy(g_own.at[owner], g_got.at[d], g1_s.at[owner], g1_r.at[d], here).wait_send()
    cot.sent()
    ua.sent()
    ub.sent()


def vmem():
    return pl.BlockSpec(memory_space=pltpu.VMEM)


def core(query, keys, values, frames, w_glu, w_out, cot, taps, norm_gain, conv_gain):
    rows, width = query.shape
    length = rows * N
    kernel = taps.shape[0]
    lanes = 128
    packed = HD + HD // 2
    dma = pltpu.SemaphoreType.DMA
    V = pltpu.VMEM
    return pl.pallas_call(
        core_kernel,
        out_shape=(
            jax.ShapeDtypeStruct((HD, 2 * width), BF16),
            jax.ShapeDtypeStruct((HD, width), BF16),
            jax.ShapeDtypeStruct((kernel, lanes), F32),
        ),
        in_specs=[vmem()] * 10,
        out_specs=(vmem(), vmem(), vmem()),
        scratch_shapes=[
            V((N, 2 * HD, rows), BF16),
            V((N, 2 * HD, rows), BF16),
            V((N, 2 * HD, rows), BF16),
            V((N, 2 * HD, rows), BF16),
            V((length, HD), BF16),
            V((HD, length), BF16),
            V((HD, length), F32),
            V((N, 2, length // 2), F32),
            V((N, 2, length // 2), F32),
            V((N, 2, length), F32),
            V((N, 2, length), F32),
            V((N, HD, 2 * HD), BF16),
            V((4, 4, HD, 2 * HD), BF16),
            V((2, N, HD, length // 2), BF16),
            V((N, rows, width), BF16),
            V((width, 128), F32),
            V((kernel, lanes), F32),
            V((2 * HD, length), F32),
            V((HD, length), F32),
            V((length + kernel, lanes), F32),
            V((length + kernel, lanes), F32),
            V((HD, length), F32),
            V((HD, length), F32),
            V((HD, length), BF16),
            V((2 * HD, length), BF16),
            V((kernel, lanes), F32),
            V((N, packed, 128), BF16),
            V((N, HD, HD), BF16),
            V((N, packed, 128), BF16),
            V((N, HD, HD), BF16),
            V((N, kernel, lanes), BF16),
            V((packed, 128), BF16),
            V((HD, HD), BF16),
            V((N, packed, 128), BF16),
            V((N, HD, HD), BF16),
        ]
        + [dma((N,))] * 14
        + [dma((15,))] * 6
        + [dma((N,))] * 10
        + [dma((4,))] * 2
        + [dma(())],
        compiler_params=pltpu.CompilerParams(
            collective_id=0, has_side_effects=True, vmem_limit_bytes=58 * 2**20
        ),
        name="core",
    )(query, keys, values, frames, w_glu, w_out, cot, taps, norm_gain, conv_gain)


def local(frames, query, keys, values, norm_gain, conv_gain, w_glu, taps, w_out, cotangent):
    glu_grad, out_grad, taps_grad = core(
        query[0], keys[0], values[0], frames[0], w_glu, w_out, cotangent[0], taps,
        norm_gain, conv_gain,
    )
    return glu_grad.astype(F32), taps_grad[:, :HD], out_grad.astype(F32)


def solution(mesh):
    return jax.shard_map(
        local,
        mesh=mesh,
        in_specs=(
            P("dp", "tm", None),
            P("dp", "tm", None),
            P("dp", "tm", None),
            P("dp", "tm", None),
            P(),
            P(),
            P("tm", None),
            P(),
            P("tm", None),
            P("dp", "tm", None),
        ),
        out_specs=(P("tm", None), P(None, "tm"), P("tm", None)),
        check_vma=False,
    )
```

```python
import functools

import jax
import jax.numpy as jnp
from jax import lax
from jax.experimental import pallas as pl
from jax.experimental.pallas import tpu as pltpu
from jax.sharding import PartitionSpec as P

N = 16
HD = 96
MESH = pl.DeviceIdType.MESH
F32 = jnp.float32
BF16 = jnp.bfloat16
EPS = 1e-05


def rem_copy(src, dst, send, recv, peer):
    return pltpu.make_async_remote_copy(
        src_ref=src, dst_ref=dst, send_sem=send, recv_sem=recv, device_id=peer, device_id_type=MESH
    )


class Gather:
    def __init__(self, me, own, out, slot, send, recv):
        self.own, self.out, self.slot, self.send, self.recv = own, out, slot, send, recv
        y = me // 4
        z = lax.rem(me // 2, 2)
        c = lax.rem(me, 2)
        at = lambda yy, zz, cc: lax.rem(yy, 4) * 4 + zz * 2 + cc
        self.me = me
        self.far = at(y, 1 - z, c)
        self.sib = at(y, z, 1 - c)
        self.to = [at(y + j, z, c) for j in range(1, 4)]
        self.frm = [at(y + 4 - j, z, c) for j in range(1, 4)]
        self.frm_far = [at(y + 4 - j, 1 - z, c) for j in range(1, 4)]
        self.frm_sib = (
            [self.sib, at(y, 1 - z, 1 - c)]
            + [at(y + 4 - j, z, 1 - c) for j in range(1, 4)]
            + [at(y + 4 - j, 1 - z, 1 - c) for j in range(1, 4)]
        )
        self.started = []

    def go(self, src, block, sem, peer):
        copy = rem_copy(
            src, self.out.at[self.slot(block)], self.send.at[sem], self.recv.at[sem], {"tm": peer}
        )
        copy.start()
        self.started.append(copy)

    def on(self, block, sem, peer):
        self.go(self.out.at[self.slot(block)], block, sem, peer)

    def landed(self, block, sem):
        ref = self.out.at[self.slot(block)]
        rem_copy(ref, ref, self.send.at[sem], self.recv.at[sem], {"tm": self.sib}).wait_recv()

    def start_far(self):
        self.go(self.own, self.me, 0, self.far)

    def start_near(self):
        for j in (0, 2, 1):
            self.go(self.own, self.me, 1 + j, self.to[j])
        self.go(self.own, self.me, 7, self.sib)

    def start(self):
        self.start_far()
        self.start_near()

    def relay_far(self):
        self.landed(self.far, 0)
        for j in (0, 2, 1):
            self.on(self.far, 4 + j, self.to[j])
        self.on(self.far, 8, self.sib)

    def relay_near(self):
        for j in (0, 2, 1):
            self.landed(self.frm[j], 1 + j)
            self.on(self.frm[j], 9 + j, self.sib)

    def relay_rest(self):
        for j in (0, 2, 1):
            self.landed(self.frm_far[j], 4 + j)
            self.on(self.frm_far[j], 12 + j, self.sib)

    def near_from_sibling(self):
        for k in (0, 2, 3, 4):
            self.landed(self.frm_sib[k], 7 + k)

    def rest_from_sibling(self):
        for k in (1, 5, 6, 7):
            self.landed(self.frm_sib[k], 7 + k)

    def sent(self):
        for copy in self.started:
            copy.wait_send()


class Swap:
    def __init__(self, me, buf, send, recv):
        self.me, self.buf, self.send, self.recv = me, buf, send, recv
        self.started = []

    def start(self):
        for i in range(1, N):
            copy = rem_copy(
                self.buf.at[self.me],
                self.buf.at[self.me],
                self.send.at[i],
                self.recv.at[i],
                {"tm": lax.rem(self.me + i, N)},
            )
            copy.start()
            self.started.append(copy)

    def finish(self):
        for i in range(1, N):
            ref = self.buf.at[lax.rem(self.me + N - i, N)]
            rem_copy(ref, ref, self.send.at[i], self.recv.at[i], {"tm": self.me}).wait_recv()
        for copy in self.started:
            copy.wait_send()


def own_stats(x):
    mean = jnp.mean(x, axis=0, keepdims=True)
    dev = x - mean
    return mean, jnp.sum(dev * dev, axis=0, keepdims=True)


def joined_stats(buf):
    means = buf[:, 0, :]
    squares = buf[:, 1, :]
    mean = jnp.mean(means, axis=0, keepdims=True)
    dev = means - mean
    total = jnp.sum(squares, axis=0, keepdims=True) + HD * jnp.sum(dev * dev, axis=0, keepdims=True)
    return mean, lax.rsqrt(total * (1.0 / (N * HD)) + EPS)


def core_kernel(
    q_ref, k_ref, v_ref, f_ref, wg_ref, wo_ref, cot_ref, taps_ref, ng_ref, cg_ref,
    glu_out, out_out, taps_out,
    kv_own, qf_own, kv, qf, k_rows, v_cols, mixed, stats_a, stats_b, stats_z, stats_e,
    w_own, w_got, u_all, cot_all, small, taps_own, p, ds, y_pad, dz_pad, z_cols, g_cols, s_cols, dp,
    t_own, g_own, o_own, g_got, o_got, t_got, g_red, o_red, g_fin, o_fin,
    kv_s, kv_r, qf_s, qf_r, w_s, w_r, st_s, st_r, sz_s, sz_r, se_s, se_r,
    sb_s, sb_r, c_s, c_r, ua_s, ua_r, ub_s, ub_r, g1_s, g1_r, o1_s, o1_r, t1_s, t1_r, g2_s, g2_r, o2_s, o2_r, wx_s, wx_r, g3_s, g3_r, own_sem,
):
    d = lax.axis_index("dp")
    t = lax.axis_index("tm")
    rows = q_ref.shape[0]
    length = mixed.shape[1]
    kernel = taps_ref.shape[0]
    half = kernel // 2
    y_at = t // 4
    group = lax.rem(t, 4)
    place = lambda block: lax.rem(block, 4) * 4 + block // 4

    barrier = pltpu.get_barrier_semaphore()

    def greet(dp_at, tm_at):
        pl.semaphore_signal(
            barrier, inc=1, device_id={"dp": dp_at, "tm": tm_at}, device_id_type=MESH
        )

    for i in range(1, N):
        greet(d, lax.rem(t + i, N))
        greet(lax.rem(d + i, N), t)
        greet(lax.rem(d + i, N), d)
        greet(t, lax.rem(t + i, N))

    @pl.when(t != d)
    def _():
        greet(d, d)
        greet(t, t)

    def turn_into(ref, buf, a):
        turned = jnp.transpose(ref[...])
        for j in range(N):
            buf[j, a * HD : (a + 1) * HD, :] = turned[j * HD : (j + 1) * HD]

    sent = []

    def scatter(src, dst, slot, send, recv):
        for i in range(1, N):
            peer = lax.rem(t + i, N)
            copy = rem_copy(src.at[peer], dst.at[slot], send.at[i], recv.at[i], {"tm": peer})
            copy.start()
            sent.append(copy)

    def arrived(dst, slot, i, send, recv):
        ref = dst.at[slot]
        rem_copy(ref, ref, send.at[i], recv.at[i], {"tm": t}).wait_recv()

    turn_into(k_ref, kv_own, 0)
    turn_into(v_ref, kv_own, 1)
    cot_keep = pltpu.make_async_copy(cot_ref, cot_all.at[t], own_sem)
    cot_keep.start()
    pl.semaphore_wait(barrier, jnp.where(t == d, 4 * (N - 1), 4 * (N - 1) + 2))
    scatter(kv_own, kv, t, kv_s, kv_r)
    turn_into(q_ref, qf_own, 0)
    turn_into(f_ref, qf_own, 1)
    scatter(qf_own, qf, t, qf_s, qf_r)
    cot = Gather(t, cot_ref, cot_all, lambda block: block, c_s, c_r)
    cot.start_near()
    width = N * HD
    for j in range(N):
        w_own[j] = jnp.concatenate(
            [
                wg_ref[:, j * HD : (j + 1) * HD],
                wg_ref[:, width + j * HD : width + (j + 1) * HD],
            ],
            axis=1,
        )
    x_at = d // 4
    for i in range(1, N):
        peer = lax.rem(t + i, N)

        @pl.when(x_at == y_at)
        def _():
            rem_copy(
                w_own.at[peer], w_got.at[y_at, group], w_s.at[i], w_r.at[group], {"tm": peer}
            ).start()

    kv[t] = kv_own[t]
    qf[t] = qf_own[t]

    @pl.when(x_at == y_at)
    def _():
        w_got[y_at, group] = w_own[t]


    small[...] = jnp.transpose(
        jnp.concatenate(
            [
                taps_ref[...],
                ng_ref[...].reshape(1, width),
                cg_ref[...].reshape(1, width),
                jnp.zeros((128 - kernel - 2, width), F32),
            ],
            axis=0,
        )
    )
    mine = small[pl.ds(pl.multiple_of(t * HD, HD), HD), :]
    lanes = taps_own.shape[1]
    blank = jnp.zeros((lanes - HD, 128), F32)
    taps_own[...] = jnp.transpose(jnp.concatenate([mine, blank], axis=0))[0:kernel]
    norm_gain = mine[:, kernel : kernel + 1]
    conv_gain = mine[:, kernel + 1 : kernel + 2]
    edge = jnp.zeros((half, lanes), F32)
    for pad in (y_pad, dz_pad):
        pad[0:half, :] = edge
        pad[length + half : length + 2 * half, :] = edge

    for i in range(1, N):
        arrived(kv, lax.rem(t + N - i, N), i, kv_s, kv_r)
    for s in range(N):
        k_rows[s * rows : (s + 1) * rows, :] = jnp.transpose(kv[s, 0:HD, :])
        v_cols[:, s * rows : (s + 1) * rows] = kv[s, HD : 2 * HD, :]
    factor = HD ** -0.5 * 1.4426950408889634
    pair = 2
    middle = length // 2

    def attend(low, high, h, stats):
        @pl.loop(low, high)
        def _(i):
            for j in range(pair):
                s = i * pair + j

                @pl.when(s != t)
                def _():
                    arrived(qf, s, lax.rem(t + N - s, N), qf_s, qf_r)

            queries = jnp.concatenate([qf[i * pair + j, 0:HD, :] for j in range(pair)], axis=1)
            field = jnp.concatenate([qf[i * pair + j, HD : 2 * HD, :] for j in range(pair)], axis=1)
            scores = jnp.dot(k_rows[...], queries, preferred_element_type=F32)
            top = jnp.max(scores, axis=0, keepdims=True)
            expo = jnp.exp2(scores * factor - top * factor)
            total = jnp.sum(expo, axis=0, keepdims=True)
            summed = jnp.dot(v_cols[...], expo.astype(BF16), preferred_element_type=F32)
            attention = (summed / total).astype(BF16)
            block = field.astype(F32) + attention.astype(F32)
            span = pair * rows
            mixed[:, pl.ds(pl.multiple_of(i * span, span), span)] = block
            cols = pl.ds(pl.multiple_of((i - h * (middle // span)) * span, span), span)
            mean, square = own_stats(block)
            stats[t, 0:1, cols] = mean
            stats[t, 1:2, cols] = square

    def make_u(h, stats, send, recv):
        mean, inv = joined_stats(stats)
        v = mixed[:, h * middle : (h + 1) * middle]
        u_all[h, place(t)] = ((v - mean) * inv * norm_gain).astype(BF16)
        gather = Gather(t, u_all.at[h, place(t)], u_all.at[h], place, send, recv)
        gather.start()
        return gather

    attend(0, 4, 0, stats_a)
    swap_a = Swap(t, stats_a, st_s, st_r)
    swap_a.start()
    attend(4, 6, 1, stats_b)
    swap_a.finish()
    ua = make_u(0, stats_a, ua_s, ua_r)
    attend(6, 8, 1, stats_b)
    swap_b = Swap(t, stats_b, sb_s, sb_r)
    swap_b.start()
    for g in range(4):

        @pl.when(x_at * 4 + g != t)
        def _():
            ref = w_got.at[x_at, g]
            rem_copy(ref, ref, w_s.at[0], w_r.at[g], {"tm": t}).wait_recv()

    for i in range(1, 4):
        ref = w_got.at[x_at]
        copy = rem_copy(
            ref, ref, wx_s.at[i], wx_r.at[i], {"dp": lax.rem(d + 4 * i, N), "tm": t}
        )
        copy.start()
        sent.append(copy)
    swap_b.finish()
    ub = make_u(1, stats_b, ub_s, ub_r)
    ua.relay_far()
    ua.relay_near()
    cot.start_far()
    cot.relay_near()

    def back_rows(z):
        @pl.loop(0, 4)
        def _(yy):
            first = yy * 4 + z * 2
            block = cot_all[pl.ds(first, 2)].reshape(2 * rows, width)
            ds[:, pl.ds(pl.multiple_of(first * rows, 2 * rows), 2 * rows)] = lax.dot_general(
                wo_ref[...], block, (((1,), (1,)), ((), ())), preferred_element_type=F32
            )

    z_at = lax.rem(t // 2, 2)
    for i in range(1, 4):
        ref = w_got.at[lax.rem(x_at + 4 - i, 4)]
        rem_copy(ref, ref, wx_s.at[i], wx_r.at[i], {"tm": t}).wait_recv()
    chunk = 512

    def product(g, h, first):
        weights = w_got[:, pl.ds(g, 1)].reshape(4 * HD, 2 * HD)

        @pl.loop(0, middle // chunk)
        def _(i):
            cols = pl.ds(pl.multiple_of(i * chunk, chunk), chunk)
            part = u_all[h, pl.ds(g * 4, 4), :, cols].reshape(4 * HD, chunk)
            part = lax.dot_general(
                weights, part, (((0,), (0,)), ((), ())), preferred_element_type=F32
            )
            cols = pl.ds(pl.multiple_of(h * middle + i * chunk, chunk), chunk)
            p[:, cols] = part if first else p[:, cols] + part

    step = 128
    blocks = length // step

    def gate(low, high):
        @pl.loop(low, high)
        def _(i):
            cols = pl.ds(pl.multiple_of(i * step, step), step)
            y = p[0:HD, cols] * jax.nn.sigmoid(p[HD : 2 * HD, cols])
            y = y.astype(BF16).astype(F32)
            y_pad[pl.ds(pl.multiple_of(half + i * step, half), step), :] = jnp.transpose(
                jnp.concatenate([y, blank], axis=0)
            )

    def conv(low, high):
        @pl.loop(low, high)
        def _(i):
            start = pl.multiple_of(i * step, step)
            z = jnp.zeros((step, lanes), F32)
            for k in range(kernel):
                z = z + taps_own[k : k + 1, :] * y_pad[pl.ds(start + k, step), :]
            z = jnp.transpose(z)[0:HD]
            cols = pl.ds(start, step)
            z_cols[:, cols] = z
            mean, square = own_stats(z)
            stats_z[t, 0:1, cols] = mean
            stats_z[t, 1:2, cols] = square

    side = lax.rem(group + 1, 2) - lax.rem(group, 2)
    other = lax.rem(group + 2, 4)
    product(group, 0, True)
    ua.near_from_sibling()
    product(group + side, 0, False)
    ub.relay_far()
    ub.relay_near()
    ua.relay_rest()
    cot.relay_far()
    cot.near_from_sibling()
    cot_keep.wait()
    back_rows(z_at)
    product(other, 0, False)
    ua.rest_from_sibling()
    product(other + side, 0, False)
    gate(0, blocks // 2)
    product(group, 1, True)
    ub.near_from_sibling()
    product(group + side, 1, False)
    conv(0, blocks // 2 - 1)
    ub.relay_rest()
    product(other, 1, False)
    ub.rest_from_sibling()
    product(other + side, 1, False)
    gate(blocks // 2, blocks)
    conv(blocks // 2 - 1, blocks)

    swap = Swap(t, stats_z, sz_s, sz_r)
    swap.start()
    cot.relay_rest()
    cot.rest_from_sibling()
    back_rows(1 - z_at)
    swap.finish()
    mean, inv = joined_stats(stats_z)
    zhat = (z_cols[...] - mean) * inv
    z_cols[...] = zhat
    n = zhat * conv_gain
    sgate = jax.nn.sigmoid(n)
    s_cols[...] = (n * sgate).astype(BF16)
    e = ds[...] * sgate * (1.0 + n * (1.0 - sgate)) * conv_gain
    g_cols[...] = e
    stats_e[t, 0:1, :] = jnp.sum(e, axis=0, keepdims=True)
    stats_e[t, 1:2, :] = jnp.sum(e * zhat, axis=0, keepdims=True)
    swap_e = Swap(t, stats_e, se_s, se_r)
    swap_e.start()

    for j in range(4):
        cols = slice(j * 4 * HD, (j + 1) * 4 * HD)
        part = jnp.dot(
            s_cols[...], cot_all[:, :, cols].reshape(length, 4 * HD), preferred_element_type=F32
        ).astype(BF16)
        for k in range(4):
            o_own[4 * j + k] = part[:, k * HD : (k + 1) * HD]
    for i in range(1, N):
        peer = lax.rem(d + i, N)
        copy = rem_copy(o_own.at[peer], o_got.at[d], o1_s.at[i], o1_r.at[i], {"dp": peer, "tm": t})
        copy.start()
        sent.append(copy)
    o_got[d] = o_own[d]

    swap_e.finish()
    sums = jnp.sum(stats_e[...], axis=0) * (1.0 / (N * HD))
    g_cols[...] = (
        ((g_cols[...] - sums[0:1] - z_cols[...] * sums[1:2]) * inv).astype(BF16).astype(F32)
    )

    @pl.loop(0, blocks)
    def turn(i):
        cols = pl.ds(pl.multiple_of(i * step, step), step)
        dz_pad[pl.ds(pl.multiple_of(half + i * step, half), step), :] = jnp.transpose(
            jnp.concatenate([g_cols[:, cols], blank], axis=0)
        )

    @pl.loop(0, blocks)
    def back(i):
        start = pl.multiple_of(i * step, step)
        dy = jnp.zeros((step, lanes), F32)
        for k in range(kernel):
            dy = dy + taps_own[k : k + 1, :] * dz_pad[pl.ds(start + 2 * half - k, step), :]
        dy = jnp.transpose(dy)[0:HD]
        cols = pl.ds(start, step)
        pa = p[0:HD, cols]
        sig = jax.nn.sigmoid(p[HD : 2 * HD, cols])
        dp[0:HD, cols] = (dy * sig).astype(BF16)
        dp[HD : 2 * HD, cols] = (dy * pa * sig * (1.0 - sig)).astype(BF16)

    @pl.loop(0, 4)
    def grads(i):
        g = lax.rem(i + d, 4)
        part = [
            lax.dot_general(
                u_all[h, pl.ds(g * 4, 4)].reshape(4 * HD, middle),
                dp[:, h * middle : (h + 1) * middle],
                (((1,), (1,)), ((), ())),
                preferred_element_type=F32,
            )
            for h in range(2)
        ]
        part = (part[0] + part[1]).astype(BF16)
        for j in range(4):
            block = part[j * HD : (j + 1) * HD]
            owner = 4 * j + g
            g_own[owner, 0:HD, :] = block[:, 0:128]
            g_own[owner, HD : HD + HD // 2, :] = jnp.concatenate(
                [block[0 : HD // 2, 128:], block[HD // 2 :, 128:]], axis=1
            )

            @pl.when(owner != d)
            def _():
                rem_copy(
                    g_own.at[owner], g_got.at[d], g1_s.at[owner], g1_r.at[d], {"dp": owner, "tm": t}
                ).start()

    g_got[d] = g_own[d]
    t_own[...] = jnp.zeros_like(t_own)

    @pl.loop(0, blocks)
    def tap_grads(i):
        start = pl.multiple_of(i * step, step)
        dz = dz_pad[pl.ds(pl.multiple_of(half + start, half), step), :]
        for k in range(kernel):
            prod = dz * y_pad[pl.ds(start + k, step), :]
            t_own[k : k + 1, :] += jnp.sum(prod, axis=0, keepdims=True)

    t_got[d] = t_own[...].astype(BF16)
    for i in range(1, N):
        peer = lax.rem(d + i, N)
        copy = rem_copy(t_got.at[d], t_got.at[d], t1_s.at[i], t1_r.at[i], {"dp": peer, "tm": t})
        copy.start()
        sent.append(copy)

    here = {"dp": d, "tm": t}

    def dp_arrived(buf, slot, send, recv, i):
        ref = buf.at[slot]
        rem_copy(ref, ref, send.at[i], recv.at[i], here).wait_recv()

    for i in range(1, N):
        slot = lax.rem(d + i, N)
        dp_arrived(g_got, slot, g1_s, g1_r, slot)
    g_red[...] = jnp.sum(g_got[...].astype(F32), axis=0).astype(BF16)
    g_slot = g_fin.at[t]
    for i in range(4):
        at_dp = y_at * 4 + lax.rem(d + i, 4)

        @pl.when(jnp.logical_or(t != d, at_dp != d))
        def _():
            rem_copy(g_red, g_slot, g2_s.at[i], g2_r.at[group], {"dp": at_dp, "tm": d}).start()

    @pl.when(t == d)
    def _():
        g_fin[t] = g_red[...]

    for k in range(4):
        s = x_at * 4 + k

        @pl.when(jnp.logical_or(s != t, t != d))
        def _():
            dp_arrived(g_fin, s, g2_s, g2_r, k)

    mine = g_fin.at[pl.ds(x_at * 4, 4)]
    for i in (1, 3, 2):
        copy = rem_copy(
            mine, mine, g3_s.at[i], g3_r.at[i], {"dp": lax.rem(d + 4 * i, N), "tm": t}
        )
        copy.start()
        sent.append(copy)

    for i in range(1, N):
        dp_arrived(o_got, lax.rem(d + N - i, N), o1_s, o1_r, i)
    o_red[...] = jnp.sum(o_got[...].astype(F32), axis=0).astype(BF16)
    for i in range(1, N):
        peer = lax.rem(d + i, N)
        copy = rem_copy(o_red, o_fin.at[d], o2_s.at[i], o2_r.at[i], {"dp": peer, "tm": t})
        copy.start()
        sent.append(copy)
    o_fin[d] = o_red[...]

    for i in range(1, N):
        dp_arrived(t_got, lax.rem(d + N - i, N), t1_s, t1_r, i)
        dp_arrived(o_fin, lax.rem(d + N - i, N), o2_s, o2_r, i)
    taps_out[...] = jnp.sum(t_got[...].astype(F32), axis=0)
    for j in range(4):
        out_out[:, j * 4 * HD : (j + 1) * 4 * HD] = jnp.concatenate(
            [o_fin[4 * j + k] for k in range(4)], axis=1
        )

    for i in range(1, 4):
        ref = g_fin.at[pl.ds(lax.rem(x_at + 4 - i, 4) * 4, 4)]
        rem_copy(ref, ref, g3_s.at[i], g3_r.at[i], here).wait_recv()

    for j in range(4):
        first, second = [], []
        for k in range(4):
            s = 4 * j + k
            wide = g_fin[s, 0:HD, :]
            tail = g_fin[s, HD : HD + HD // 2, :]
            first.append(wide[:, 0:HD])
            second.append(wide[:, HD:])
            second.append(jnp.concatenate([tail[:, 0:64], tail[:, 64:]], axis=0))
        cols = slice(j * 4 * HD, (j + 1) * 4 * HD)
        glu_out[:, cols] = jnp.concatenate(first, axis=1)
        cols = slice(width + j * 4 * HD, width + (j + 1) * 4 * HD)
        glu_out[:, cols] = jnp.concatenate(second, axis=1)

    for i in range(4):
        at_dp = y_at * 4 + lax.rem(d + i, 4)

        @pl.when(jnp.logical_or(t != d, at_dp != d))
        def _():
            rem_copy(g_red, g_slot, g2_s.at[i], g2_r.at[group], here).wait_send()

    for copy in sent:
        copy.wait_send()
    for i in range(1, N):

        @pl.when(x_at == y_at)
        def _():
            ref = w_own.at[lax.rem(t + i, N)]
            rem_copy(ref, ref, w_s.at[i], w_r.at[group], {"tm": t}).wait_send()

    for i in range(1, N):
        owner = lax.rem(d + i, N)
        rem_copy(g_own.at[owner], g_got.at[d], g1_s.at[owner], g1_r.at[d], here).wait_send()
    cot.sent()
    ua.sent()
    ub.sent()


def vmem():
    return pl.BlockSpec(memory_space=pltpu.VMEM)


def core(query, keys, values, frames, w_glu, w_out, cot, taps, norm_gain, conv_gain):
    rows, width = query.shape
    length = rows * N
    kernel = taps.shape[0]
    lanes = 128
    packed = HD + HD // 2
    dma = pltpu.SemaphoreType.DMA
    V = pltpu.VMEM
    return pl.pallas_call(
        core_kernel,
        out_shape=(
            jax.ShapeDtypeStruct((HD, 2 * width), BF16),
            jax.ShapeDtypeStruct((HD, width), BF16),
            jax.ShapeDtypeStruct((kernel, lanes), F32),
        ),
        in_specs=[vmem()] * 10,
        out_specs=(vmem(), vmem(), vmem()),
        scratch_shapes=[
            V((N, 2 * HD, rows), BF16),
            V((N, 2 * HD, rows), BF16),
            V((N, 2 * HD, rows), BF16),
            V((N, 2 * HD, rows), BF16),
            V((length, HD), BF16),
            V((HD, length), BF16),
            V((HD, length), F32),
            V((N, 2, length // 2), F32),
            V((N, 2, length // 2), F32),
            V((N, 2, length), F32),
            V((N, 2, length), F32),
            V((N, HD, 2 * HD), BF16),
            V((4, 4, HD, 2 * HD), BF16),
            V((2, N, HD, length // 2), BF16),
            V((N, rows, width), BF16),
            V((width, 128), F32),
            V((kernel, lanes), F32),
            V((2 * HD, length), F32),
            V((HD, length), F32),
            V((length + kernel, lanes), F32),
            V((length + kernel, lanes), F32),
            V((HD, length), F32),
            V((HD, length), F32),
            V((HD, length), BF16),
            V((2 * HD, length), BF16),
            V((kernel, lanes), F32),
            V((N, packed, 128), BF16),
            V((N, HD, HD), BF16),
            V((N, packed, 128), BF16),
            V((N, HD, HD), BF16),
            V((N, kernel, lanes), BF16),
            V((packed, 128), BF16),
            V((HD, HD), BF16),
            V((N, packed, 128), BF16),
            V((N, HD, HD), BF16),
        ]
        + [dma((N,))] * 14
        + [dma((15,))] * 6
        + [dma((N,))] * 10
        + [dma((4,))] * 4
        + [dma(())],
        compiler_params=pltpu.CompilerParams(
            collective_id=0, has_side_effects=True, vmem_limit_bytes=58 * 2**20
        ),
        name="core",
    )(query, keys, values, frames, w_glu, w_out, cot, taps, norm_gain, conv_gain)


def local(frames, query, keys, values, norm_gain, conv_gain, w_glu, taps, w_out, cotangent):
    glu_grad, out_grad, taps_grad = core(
        query[0], keys[0], values[0], frames[0], w_glu, w_out, cotangent[0], taps,
        norm_gain, conv_gain,
    )
    return glu_grad.astype(F32), taps_grad[:, :HD], out_grad.astype(F32)


def solution(mesh):
    return jax.shard_map(
        local,
        mesh=mesh,
        in_specs=(
            P("dp", "tm", None),
            P("dp", "tm", None),
            P("dp", "tm", None),
            P("dp", "tm", None),
            P(),
            P(),
            P("tm", None),
            P(),
            P("tm", None),
            P("dp", "tm", None),
        ),
        out_specs=(P("tm", None), P(None, "tm"), P("tm", None)),
        check_vma=False,
    )
```

```python
import functools

import jax
import jax.numpy as jnp
from jax import lax
from jax.experimental import pallas as pl
from jax.experimental.pallas import tpu as pltpu
from jax.sharding import PartitionSpec as P

N = 16
HD = 96
MESH = pl.DeviceIdType.MESH
F32 = jnp.float32
BF16 = jnp.bfloat16
EPS = 1e-05


def rem_copy(src, dst, send, recv, peer):
    return pltpu.make_async_remote_copy(
        src_ref=src, dst_ref=dst, send_sem=send, recv_sem=recv, device_id=peer, device_id_type=MESH
    )


class Gather:
    def __init__(self, me, own, out, slot, send, recv):
        self.own, self.out, self.slot, self.send, self.recv = own, out, slot, send, recv
        y = me // 4
        z = lax.rem(me // 2, 2)
        c = lax.rem(me, 2)
        at = lambda yy, zz, cc: lax.rem(yy, 4) * 4 + zz * 2 + cc
        self.me = me
        self.far = at(y, 1 - z, c)
        self.sib = at(y, z, 1 - c)
        self.to = [at(y + j, z, c) for j in range(1, 4)]
        self.frm = [at(y + 4 - j, z, c) for j in range(1, 4)]
        self.frm_far = [at(y + 4 - j, 1 - z, c) for j in range(1, 4)]
        self.frm_sib = (
            [self.sib, at(y, 1 - z, 1 - c)]
            + [at(y + 4 - j, z, 1 - c) for j in range(1, 4)]
            + [at(y + 4 - j, 1 - z, 1 - c) for j in range(1, 4)]
        )
        self.started = []

    def go(self, src, block, sem, peer):
        copy = rem_copy(
            src, self.out.at[self.slot(block)], self.send.at[sem], self.recv.at[sem], {"tm": peer}
        )
        copy.start()
        self.started.append(copy)

    def on(self, block, sem, peer):
        self.go(self.out.at[self.slot(block)], block, sem, peer)

    def landed(self, block, sem):
        ref = self.out.at[self.slot(block)]
        rem_copy(ref, ref, self.send.at[sem], self.recv.at[sem], {"tm": self.sib}).wait_recv()

    def start_far(self):
        self.go(self.own, self.me, 0, self.far)

    def start_near(self):
        for j in (0, 2, 1):
            self.go(self.own, self.me, 1 + j, self.to[j])
        self.go(self.own, self.me, 7, self.sib)

    def start(self):
        self.start_far()
        self.start_near()

    def relay_far(self):
        self.landed(self.far, 0)
        for j in (0, 2, 1):
            self.on(self.far, 4 + j, self.to[j])
        self.on(self.far, 8, self.sib)

    def relay_near(self):
        for j in (0, 2, 1):
            self.landed(self.frm[j], 1 + j)
            self.on(self.frm[j], 9 + j, self.sib)

    def relay_rest(self):
        for j in (0, 2, 1):
            self.landed(self.frm_far[j], 4 + j)
            self.on(self.frm_far[j], 12 + j, self.sib)

    def near_from_sibling(self):
        for k in (0, 2, 3, 4):
            self.landed(self.frm_sib[k], 7 + k)

    def rest_from_sibling(self):
        for k in (1, 5, 6, 7):
            self.landed(self.frm_sib[k], 7 + k)

    def sent(self):
        for copy in self.started:
            copy.wait_send()


class Swap:
    def __init__(self, me, buf, send, recv):
        self.me, self.buf, self.send, self.recv = me, buf, send, recv
        self.started = []

    def start(self):
        for i in range(1, N):
            copy = rem_copy(
                self.buf.at[self.me],
                self.buf.at[self.me],
                self.send.at[i],
                self.recv.at[i],
                {"tm": lax.rem(self.me + i, N)},
            )
            copy.start()
            self.started.append(copy)

    def finish(self):
        for i in range(1, N):
            ref = self.buf.at[lax.rem(self.me + N - i, N)]
            rem_copy(ref, ref, self.send.at[i], self.recv.at[i], {"tm": self.me}).wait_recv()
        for copy in self.started:
            copy.wait_send()


def own_stats(x):
    mean = jnp.mean(x, axis=0, keepdims=True)
    dev = x - mean
    return mean, jnp.sum(dev * dev, axis=0, keepdims=True)


def joined_stats(buf):
    means = buf[:, 0, :]
    squares = buf[:, 1, :]
    mean = jnp.mean(means, axis=0, keepdims=True)
    dev = means - mean
    total = jnp.sum(squares, axis=0, keepdims=True) + HD * jnp.sum(dev * dev, axis=0, keepdims=True)
    return mean, lax.rsqrt(total * (1.0 / (N * HD)) + EPS)


def core_kernel(
    q_in, k_ref, v_ref, f_in, wg_in, wo_in, cot_ref, taps_ref, ng_ref, cg_ref,
    glu_out, out_out, taps_out,
    kv_own, qf_own, kv, qf, k_rows, v_cols, mixed, stats_a, stats_b, stats_z, stats_e,
    w_own, w_got, u_all, cot_all, small, taps_own, p, ds, y_pad, dz_pad, z_cols, g_cols, s_cols, dp,
    t_own, g_own, o_own, g_got, o_got, t_got, g_red, o_red, g_fin, o_fin,
    kv_s, kv_r, qf_s, qf_r, w_s, w_r, st_s, st_r, sz_s, sz_r, se_s, se_r,
    sb_s, sb_r, c_s, c_r, ua_s, ua_r, ub_s, ub_r, g1_s, g1_r, o1_s, o1_r, t1_s, t1_r, g2_s, g2_r, o2_s, o2_r, wx_s, wx_r, g3_s, g3_r, load_sem, own_sem,
    q_ref, f_ref, wg_ref, wo_ref,
):
    d = lax.axis_index("dp")
    t = lax.axis_index("tm")
    rows = k_ref.shape[0]
    length = mixed.shape[1]
    kernel = taps_ref.shape[0]
    half = kernel // 2
    y_at = t // 4
    group = lax.rem(t, 4)
    place = lambda block: lax.rem(block, 4) * 4 + block // 4

    barrier = pltpu.get_barrier_semaphore()

    def greet(dp_at, tm_at):
        pl.semaphore_signal(
            barrier, inc=1, device_id={"dp": dp_at, "tm": tm_at}, device_id_type=MESH
        )

    for i in range(1, N):
        greet(d, lax.rem(t + i, N))
        greet(lax.rem(d + i, N), t)
        greet(lax.rem(d + i, N), d)
        greet(t, lax.rem(t + i, N))

    @pl.when(t != d)
    def _():
        greet(d, d)
        greet(t, t)

    def turn_into(ref, buf, a):
        turned = jnp.transpose(ref[...])
        for j in range(N):
            buf[j, a * HD : (a + 1) * HD, :] = turned[j * HD : (j + 1) * HD]

    sent = []

    def scatter(src, dst, slot, send, recv):
        for i in range(1, N):
            peer = lax.rem(t + i, N)
            copy = rem_copy(src.at[peer], dst.at[slot], send.at[i], recv.at[i], {"tm": peer})
            copy.start()
            sent.append(copy)

    def arrived(dst, slot, i, send, recv):
        ref = dst.at[slot]
        rem_copy(ref, ref, send.at[i], recv.at[i], {"tm": t}).wait_recv()

    loads = [
        pltpu.make_async_copy(src, dst, load_sem.at[i])
        for i, (src, dst) in enumerate(
            ((q_in, q_ref), (f_in, f_ref), (wg_in, wg_ref), (wo_in, wo_ref))
        )
    ]
    for load in loads:
        load.start()
    turn_into(k_ref, kv_own, 0)
    turn_into(v_ref, kv_own, 1)
    cot_keep = pltpu.make_async_copy(cot_ref, cot_all.at[t], own_sem)
    cot_keep.start()
    pl.semaphore_wait(barrier, jnp.where(t == d, 4 * (N - 1), 4 * (N - 1) + 2))
    scatter(kv_own, kv, t, kv_s, kv_r)
    for load in loads:
        load.wait()
    turn_into(q_ref, qf_own, 0)
    turn_into(f_ref, qf_own, 1)
    scatter(qf_own, qf, t, qf_s, qf_r)
    cot = Gather(t, cot_ref, cot_all, lambda block: block, c_s, c_r)
    cot.start_near()
    width = N * HD
    for j in range(N):
        w_own[j] = jnp.concatenate(
            [
                wg_ref[:, j * HD : (j + 1) * HD],
                wg_ref[:, width + j * HD : width + (j + 1) * HD],
            ],
            axis=1,
        )
    x_at = d // 4
    for i in range(1, N):
        peer = lax.rem(t + i, N)

        @pl.when(x_at == y_at)
        def _():
            rem_copy(
                w_own.at[peer], w_got.at[y_at, group], w_s.at[i], w_r.at[group], {"tm": peer}
            ).start()

    kv[t] = kv_own[t]
    qf[t] = qf_own[t]

    @pl.when(x_at == y_at)
    def _():
        w_got[y_at, group] = w_own[t]


    small[...] = jnp.transpose(
        jnp.concatenate(
            [
                taps_ref[...],
                ng_ref[...].reshape(1, width),
                cg_ref[...].reshape(1, width),
                jnp.zeros((128 - kernel - 2, width), F32),
            ],
            axis=0,
        )
    )
    mine = small[pl.ds(pl.multiple_of(t * HD, HD), HD), :]
    lanes = taps_own.shape[1]
    blank = jnp.zeros((lanes - HD, 128), F32)
    taps_own[...] = jnp.transpose(jnp.concatenate([mine, blank], axis=0))[0:kernel]
    norm_gain = mine[:, kernel : kernel + 1]
    conv_gain = mine[:, kernel + 1 : kernel + 2]
    edge = jnp.zeros((half, lanes), F32)
    for pad in (y_pad, dz_pad):
        pad[0:half, :] = edge
        pad[length + half : length + 2 * half, :] = edge

    for i in range(1, N):
        arrived(kv, lax.rem(t + N - i, N), i, kv_s, kv_r)
    for s in range(N):
        k_rows[s * rows : (s + 1) * rows, :] = jnp.transpose(kv[s, 0:HD, :])
        v_cols[:, s * rows : (s + 1) * rows] = kv[s, HD : 2 * HD, :]
    factor = HD ** -0.5 * 1.4426950408889634
    pair = 2
    middle = length // 2

    def attend(low, high, h, stats):
        @pl.loop(low, high)
        def _(i):
            for j in range(pair):
                s = i * pair + j

                @pl.when(s != t)
                def _():
                    arrived(qf, s, lax.rem(t + N - s, N), qf_s, qf_r)

            queries = jnp.concatenate([qf[i * pair + j, 0:HD, :] for j in range(pair)], axis=1)
            field = jnp.concatenate([qf[i * pair + j, HD : 2 * HD, :] for j in range(pair)], axis=1)
            scores = jnp.dot(k_rows[...], queries, preferred_element_type=F32)
            top = jnp.max(scores, axis=0, keepdims=True)
            expo = jnp.exp2(scores * factor - top * factor)
            total = jnp.sum(expo, axis=0, keepdims=True)
            summed = jnp.dot(v_cols[...], expo.astype(BF16), preferred_element_type=F32)
            attention = (summed / total).astype(BF16)
            block = field.astype(F32) + attention.astype(F32)
            span = pair * rows
            mixed[:, pl.ds(pl.multiple_of(i * span, span), span)] = block
            cols = pl.ds(pl.multiple_of((i - h * (middle // span)) * span, span), span)
            mean, square = own_stats(block)
            stats[t, 0:1, cols] = mean
            stats[t, 1:2, cols] = square

    def make_u(h, stats, send, recv):
        mean, inv = joined_stats(stats)
        v = mixed[:, h * middle : (h + 1) * middle]
        u_all[h, place(t)] = ((v - mean) * inv * norm_gain).astype(BF16)
        gather = Gather(t, u_all.at[h, place(t)], u_all.at[h], place, send, recv)
        gather.start()
        return gather

    attend(0, 4, 0, stats_a)
    swap_a = Swap(t, stats_a, st_s, st_r)
    swap_a.start()
    attend(4, 6, 1, stats_b)
    swap_a.finish()
    ua = make_u(0, stats_a, ua_s, ua_r)
    attend(6, 8, 1, stats_b)
    swap_b = Swap(t, stats_b, sb_s, sb_r)
    swap_b.start()
    for g in range(4):

        @pl.when(x_at * 4 + g != t)
        def _():
            ref = w_got.at[x_at, g]
            rem_copy(ref, ref, w_s.at[0], w_r.at[g], {"tm": t}).wait_recv()

    for i in range(1, 4):
        ref = w_got.at[x_at]
        copy = rem_copy(
            ref, ref, wx_s.at[i], wx_r.at[i], {"dp": lax.rem(d + 4 * i, N), "tm": t}
        )
        copy.start()
        sent.append(copy)
    swap_b.finish()
    ub = make_u(1, stats_b, ub_s, ub_r)
    ua.relay_far()
    ua.relay_near()
    cot.start_far()
    cot.relay_near()

    def back_rows(z):
        @pl.loop(0, 4)
        def _(yy):
            first = yy * 4 + z * 2
            block = cot_all[pl.ds(first, 2)].reshape(2 * rows, width)
            ds[:, pl.ds(pl.multiple_of(first * rows, 2 * rows), 2 * rows)] = lax.dot_general(
                wo_ref[...], block, (((1,), (1,)), ((), ())), preferred_element_type=F32
            )

    z_at = lax.rem(t // 2, 2)
    for i in range(1, 4):
        ref = w_got.at[lax.rem(x_at + 4 - i, 4)]
        rem_copy(ref, ref, wx_s.at[i], wx_r.at[i], {"tm": t}).wait_recv()
    chunk = 512

    def product(g, h, first):
        weights = w_got[:, pl.ds(g, 1)].reshape(4 * HD, 2 * HD)

        @pl.loop(0, middle // chunk)
        def _(i):
            cols = pl.ds(pl.multiple_of(i * chunk, chunk), chunk)
            part = u_all[h, pl.ds(g * 4, 4), :, cols].reshape(4 * HD, chunk)
            part = lax.dot_general(
                weights, part, (((0,), (0,)), ((), ())), preferred_element_type=F32
            )
            cols = pl.ds(pl.multiple_of(h * middle + i * chunk, chunk), chunk)
            p[:, cols] = part if first else p[:, cols] + part

    step = 128
    blocks = length // step

    def gate(low, high):
        @pl.loop(low, high)
        def _(i):
            cols = pl.ds(pl.multiple_of(i * step, step), step)
            y = p[0:HD, cols] * jax.nn.sigmoid(p[HD : 2 * HD, cols])
            y = y.astype(BF16).astype(F32)
            y_pad[pl.ds(pl.multiple_of(half + i * step, half), step), :] = jnp.transpose(
                jnp.concatenate([y, blank], axis=0)
            )

    def conv(low, high):
        @pl.loop(low, high)
        def _(i):
            start = pl.multiple_of(i * step, step)
            z = jnp.zeros((step, lanes), F32)
            for k in range(kernel):
                z = z + taps_own[k : k + 1, :] * y_pad[pl.ds(start + k, step), :]
            z = jnp.transpose(z)[0:HD]
            cols = pl.ds(start, step)
            z_cols[:, cols] = z
            mean, square = own_stats(z)
            stats_z[t, 0:1, cols] = mean
            stats_z[t, 1:2, cols] = square

    side = lax.rem(group + 1, 2) - lax.rem(group, 2)
    other = lax.rem(group + 2, 4)
    product(group, 0, True)
    ua.near_from_sibling()
    product(group + side, 0, False)
    ub.relay_far()
    ub.relay_near()
    ua.relay_rest()
    cot.relay_far()
    cot.near_from_sibling()
    cot_keep.wait()
    back_rows(z_at)
    product(other, 0, False)
    ua.rest_from_sibling()
    product(other + side, 0, False)
    gate(0, blocks // 2)
    product(group, 1, True)
    ub.near_from_sibling()
    product(group + side, 1, False)
    conv(0, blocks // 2 - 1)
    ub.relay_rest()
    product(other, 1, False)
    ub.rest_from_sibling()
    product(other + side, 1, False)
    gate(blocks // 2, blocks)
    conv(blocks // 2 - 1, blocks)

    swap = Swap(t, stats_z, sz_s, sz_r)
    swap.start()
    cot.relay_rest()
    cot.rest_from_sibling()
    back_rows(1 - z_at)
    swap.finish()
    mean, inv = joined_stats(stats_z)
    zhat = (z_cols[...] - mean) * inv
    z_cols[...] = zhat
    n = zhat * conv_gain
    sgate = jax.nn.sigmoid(n)
    s_cols[...] = (n * sgate).astype(BF16)
    e = ds[...] * sgate * (1.0 + n * (1.0 - sgate)) * conv_gain
    g_cols[...] = e
    stats_e[t, 0:1, :] = jnp.sum(e, axis=0, keepdims=True)
    stats_e[t, 1:2, :] = jnp.sum(e * zhat, axis=0, keepdims=True)
    swap_e = Swap(t, stats_e, se_s, se_r)
    swap_e.start()

    for j in range(4):
        cols = slice(j * 4 * HD, (j + 1) * 4 * HD)
        part = jnp.dot(
            s_cols[...], cot_all[:, :, cols].reshape(length, 4 * HD), preferred_element_type=F32
        ).astype(BF16)
        for k in range(4):
            o_own[4 * j + k] = part[:, k * HD : (k + 1) * HD]
    for i in range(1, N):
        peer = lax.rem(d + i, N)
        copy = rem_copy(o_own.at[peer], o_got.at[d], o1_s.at[i], o1_r.at[i], {"dp": peer, "tm": t})
        copy.start()
        sent.append(copy)
    o_got[d] = o_own[d]

    swap_e.finish()
    sums = jnp.sum(stats_e[...], axis=0) * (1.0 / (N * HD))
    g_cols[...] = (
        ((g_cols[...] - sums[0:1] - z_cols[...] * sums[1:2]) * inv).astype(BF16).astype(F32)
    )

    @pl.loop(0, blocks)
    def turn(i):
        cols = pl.ds(pl.multiple_of(i * step, step), step)
        dz_pad[pl.ds(pl.multiple_of(half + i * step, half), step), :] = jnp.transpose(
            jnp.concatenate([g_cols[:, cols], blank], axis=0)
        )

    @pl.loop(0, blocks)
    def back(i):
        start = pl.multiple_of(i * step, step)
        dy = jnp.zeros((step, lanes), F32)
        for k in range(kernel):
            dy = dy + taps_own[k : k + 1, :] * dz_pad[pl.ds(start + 2 * half - k, step), :]
        dy = jnp.transpose(dy)[0:HD]
        cols = pl.ds(start, step)
        pa = p[0:HD, cols]
        sig = jax.nn.sigmoid(p[HD : 2 * HD, cols])
        dp[0:HD, cols] = (dy * sig).astype(BF16)
        dp[HD : 2 * HD, cols] = (dy * pa * sig * (1.0 - sig)).astype(BF16)

    @pl.loop(0, 4)
    def grads(i):
        g = lax.rem(i + d, 4)
        part = [
            lax.dot_general(
                u_all[h, pl.ds(g * 4, 4)].reshape(4 * HD, middle),
                dp[:, h * middle : (h + 1) * middle],
                (((1,), (1,)), ((), ())),
                preferred_element_type=F32,
            )
            for h in range(2)
        ]
        part = (part[0] + part[1]).astype(BF16)
        for j in range(4):
            block = part[j * HD : (j + 1) * HD]
            owner = 4 * j + g
            g_own[owner, 0:HD, :] = block[:, 0:128]
            g_own[owner, HD : HD + HD // 2, :] = jnp.concatenate(
                [block[0 : HD // 2, 128:], block[HD // 2 :, 128:]], axis=1
            )

            @pl.when(owner != d)
            def _():
                rem_copy(
                    g_own.at[owner], g_got.at[d], g1_s.at[owner], g1_r.at[d], {"dp": owner, "tm": t}
                ).start()

    g_got[d] = g_own[d]
    t_own[...] = jnp.zeros_like(t_own)

    @pl.loop(0, blocks)
    def tap_grads(i):
        start = pl.multiple_of(i * step, step)
        dz = dz_pad[pl.ds(pl.multiple_of(half + start, half), step), :]
        for k in range(kernel):
            prod = dz * y_pad[pl.ds(start + k, step), :]
            t_own[k : k + 1, :] += jnp.sum(prod, axis=0, keepdims=True)

    t_got[d] = t_own[...].astype(BF16)
    for i in range(1, N):
        peer = lax.rem(d + i, N)
        copy = rem_copy(t_got.at[d], t_got.at[d], t1_s.at[i], t1_r.at[i], {"dp": peer, "tm": t})
        copy.start()
        sent.append(copy)

    here = {"dp": d, "tm": t}

    def dp_arrived(buf, slot, send, recv, i):
        ref = buf.at[slot]
        rem_copy(ref, ref, send.at[i], recv.at[i], here).wait_recv()

    for i in range(1, N):
        slot = lax.rem(d + i, N)
        dp_arrived(g_got, slot, g1_s, g1_r, slot)
    g_red[...] = jnp.sum(g_got[...].astype(F32), axis=0).astype(BF16)
    g_slot = g_fin.at[t]
    for i in range(4):
        at_dp = y_at * 4 + lax.rem(d + i, 4)

        @pl.when(jnp.logical_or(t != d, at_dp != d))
        def _():
            rem_copy(g_red, g_slot, g2_s.at[i], g2_r.at[group], {"dp": at_dp, "tm": d}).start()

    @pl.when(t == d)
    def _():
        g_fin[t] = g_red[...]

    for k in range(4):
        s = x_at * 4 + k

        @pl.when(jnp.logical_or(s != t, t != d))
        def _():
            dp_arrived(g_fin, s, g2_s, g2_r, k)

    mine = g_fin.at[pl.ds(x_at * 4, 4)]
    for i in (1, 3, 2):
        copy = rem_copy(
            mine, mine, g3_s.at[i], g3_r.at[i], {"dp": lax.rem(d + 4 * i, N), "tm": t}
        )
        copy.start()
        sent.append(copy)

    for i in range(1, N):
        dp_arrived(o_got, lax.rem(d + N - i, N), o1_s, o1_r, i)
    o_red[...] = jnp.sum(o_got[...].astype(F32), axis=0).astype(BF16)
    for i in range(1, N):
        peer = lax.rem(d + i, N)
        copy = rem_copy(o_red, o_fin.at[d], o2_s.at[i], o2_r.at[i], {"dp": peer, "tm": t})
        copy.start()
        sent.append(copy)
    o_fin[d] = o_red[...]

    for i in range(1, N):
        dp_arrived(t_got, lax.rem(d + N - i, N), t1_s, t1_r, i)
        dp_arrived(o_fin, lax.rem(d + N - i, N), o2_s, o2_r, i)
    taps_out[...] = jnp.sum(t_got[...].astype(F32), axis=0)
    for j in range(4):
        out_out[:, j * 4 * HD : (j + 1) * 4 * HD] = jnp.concatenate(
            [o_fin[4 * j + k] for k in range(4)], axis=1
        )

    for i in (0, 1, 3, 2):
        j = lax.rem(x_at + 4 - i, 4)
        if i > 0:
            ref = g_fin.at[pl.ds(j * 4, 4)]
            rem_copy(ref, ref, g3_s.at[i], g3_r.at[i], here).wait_recv()
        first, second = [], []
        for k in range(4):
            s = 4 * j + k
            wide = g_fin[s, 0:HD, :]
            tail = g_fin[s, HD : HD + HD // 2, :]
            first.append(wide[:, 0:HD])
            second.append(wide[:, HD:])
            second.append(jnp.concatenate([tail[:, 0:64], tail[:, 64:]], axis=0))
        base = pl.multiple_of(j * 4 * HD, 4 * HD)
        glu_out[:, pl.ds(base, 4 * HD)] = jnp.concatenate(first, axis=1)
        base = pl.multiple_of(width + j * 4 * HD, 4 * HD)
        glu_out[:, pl.ds(base, 4 * HD)] = jnp.concatenate(second, axis=1)

    for i in range(4):
        at_dp = y_at * 4 + lax.rem(d + i, 4)

        @pl.when(jnp.logical_or(t != d, at_dp != d))
        def _():
            rem_copy(g_red, g_slot, g2_s.at[i], g2_r.at[group], here).wait_send()

    for copy in sent:
        copy.wait_send()
    for i in range(1, N):

        @pl.when(x_at == y_at)
        def _():
            ref = w_own.at[lax.rem(t + i, N)]
            rem_copy(ref, ref, w_s.at[i], w_r.at[group], {"tm": t}).wait_send()

    for i in range(1, N):
        owner = lax.rem(d + i, N)
        rem_copy(g_own.at[owner], g_got.at[d], g1_s.at[owner], g1_r.at[d], here).wait_send()
    cot.sent()
    ua.sent()
    ub.sent()


def anywhere():
    return pl.BlockSpec(memory_space=pl.ANY)


def vmem():
    return pl.BlockSpec(memory_space=pltpu.VMEM)


def core(query, keys, values, frames, w_glu, w_out, cot, taps, norm_gain, conv_gain):
    rows, width = query.shape
    length = rows * N
    kernel = taps.shape[0]
    lanes = 128
    packed = HD + HD // 2
    dma = pltpu.SemaphoreType.DMA
    V = pltpu.VMEM
    return pl.pallas_call(
        core_kernel,
        out_shape=(
            jax.ShapeDtypeStruct((HD, 2 * width), BF16),
            jax.ShapeDtypeStruct((HD, width), BF16),
            jax.ShapeDtypeStruct((kernel, lanes), F32),
        ),
        in_specs=[anywhere(), vmem(), vmem()] + [anywhere()] * 4 + [vmem()] * 3,
        out_specs=(vmem(), vmem(), vmem()),
        scratch_shapes=[
            V((N, 2 * HD, rows), BF16),
            V((N, 2 * HD, rows), BF16),
            V((N, 2 * HD, rows), BF16),
            V((N, 2 * HD, rows), BF16),
            V((length, HD), BF16),
            V((HD, length), BF16),
            V((HD, length), F32),
            V((N, 2, length // 2), F32),
            V((N, 2, length // 2), F32),
            V((N, 2, length), F32),
            V((N, 2, length), F32),
            V((N, HD, 2 * HD), BF16),
            V((4, 4, HD, 2 * HD), BF16),
            V((2, N, HD, length // 2), BF16),
            V((N, rows, width), BF16),
            V((width, 128), F32),
            V((kernel, lanes), F32),
            V((2 * HD, length), F32),
            V((HD, length), F32),
            V((length + kernel, lanes), F32),
            V((length + kernel, lanes), F32),
            V((HD, length), F32),
            V((HD, length), F32),
            V((HD, length), BF16),
            V((2 * HD, length), BF16),
            V((kernel, lanes), F32),
            V((N, packed, 128), BF16),
            V((N, HD, HD), BF16),
            V((N, packed, 128), BF16),
            V((N, HD, HD), BF16),
            V((N, kernel, lanes), BF16),
            V((packed, 128), BF16),
            V((HD, HD), BF16),
            V((N, packed, 128), BF16),
            V((N, HD, HD), BF16),
        ]
        + [dma((N,))] * 14
        + [dma((15,))] * 6
        + [dma((N,))] * 10
        + [dma((4,))] * 5
        + [dma(())]
        + [
            V((rows, width), BF16),
            V((rows, width), BF16),
            V((HD, 2 * width), BF16),
            V((HD, width), BF16),
        ],
        compiler_params=pltpu.CompilerParams(
            collective_id=0, has_side_effects=True, vmem_limit_bytes=58 * 2**20
        ),
        name="core",
    )(query, keys, values, frames, w_glu, w_out, cot, taps, norm_gain, conv_gain)


def local(frames, query, keys, values, norm_gain, conv_gain, w_glu, taps, w_out, cotangent):
    glu_grad, out_grad, taps_grad = core(
        query[0], keys[0], values[0], frames[0], w_glu, w_out, cotangent[0], taps,
        norm_gain, conv_gain,
    )
    return glu_grad.astype(F32), taps_grad[:, :HD], out_grad.astype(F32)


def solution(mesh):
    return jax.shard_map(
        local,
        mesh=mesh,
        in_specs=(
            P("dp", "tm", None),
            P("dp", "tm", None),
            P("dp", "tm", None),
            P("dp", "tm", None),
            P(),
            P(),
            P("tm", None),
            P(),
            P("tm", None),
            P("dp", "tm", None),
        ),
        out_specs=(P("tm", None), P(None, "tm"), P("tm", None)),
        check_vma=False,
    )
```

```python
import functools

import jax
import jax.numpy as jnp
from jax import lax
from jax.experimental import pallas as pl
from jax.experimental.pallas import tpu as pltpu
from jax.sharding import PartitionSpec as P

N = 16
HD = 96
MESH = pl.DeviceIdType.MESH
F32 = jnp.float32
BF16 = jnp.bfloat16
EPS = 1e-05


def rem_copy(src, dst, send, recv, peer):
    return pltpu.make_async_remote_copy(
        src_ref=src, dst_ref=dst, send_sem=send, recv_sem=recv, device_id=peer, device_id_type=MESH
    )


class Gather:
    def __init__(self, me, own, out, slot, send, recv):
        self.own, self.out, self.slot, self.send, self.recv = own, out, slot, send, recv
        y = me // 4
        z = lax.rem(me // 2, 2)
        c = lax.rem(me, 2)
        at = lambda yy, zz, cc: lax.rem(yy, 4) * 4 + zz * 2 + cc
        self.me = me
        self.far = at(y, 1 - z, c)
        self.sib = at(y, z, 1 - c)
        self.to = [at(y + j, z, c) for j in range(1, 4)]
        self.frm = [at(y + 4 - j, z, c) for j in range(1, 4)]
        self.frm_far = [at(y + 4 - j, 1 - z, c) for j in range(1, 4)]
        self.frm_sib = (
            [self.sib, at(y, 1 - z, 1 - c)]
            + [at(y + 4 - j, z, 1 - c) for j in range(1, 4)]
            + [at(y + 4 - j, 1 - z, 1 - c) for j in range(1, 4)]
        )
        self.started = []

    def go(self, src, block, sem, peer):
        copy = rem_copy(
            src, self.out.at[self.slot(block)], self.send.at[sem], self.recv.at[sem], {"tm": peer}
        )
        copy.start()
        self.started.append(copy)

    def on(self, block, sem, peer):
        self.go(self.out.at[self.slot(block)], block, sem, peer)

    def landed(self, block, sem):
        ref = self.out.at[self.slot(block)]
        rem_copy(ref, ref, self.send.at[sem], self.recv.at[sem], {"tm": self.sib}).wait_recv()

    def start_far(self):
        self.go(self.own, self.me, 0, self.far)

    def start_near(self):
        for j in (0, 2, 1):
            self.go(self.own, self.me, 1 + j, self.to[j])
        self.go(self.own, self.me, 7, self.sib)

    def start(self):
        self.start_far()
        self.start_near()

    def relay_far(self):
        self.landed(self.far, 0)
        for j in (0, 2, 1):
            self.on(self.far, 4 + j, self.to[j])
        self.on(self.far, 8, self.sib)

    def relay_near(self):
        for j in (0, 2, 1):
            self.landed(self.frm[j], 1 + j)
            self.on(self.frm[j], 9 + j, self.sib)

    def relay_rest(self):
        for j in (0, 2, 1):
            self.landed(self.frm_far[j], 4 + j)
            self.on(self.frm_far[j], 12 + j, self.sib)

    def near_from_sibling(self):
        for k in (0, 2, 3, 4):
            self.landed(self.frm_sib[k], 7 + k)

    def rest_from_sibling(self):
        for k in (1, 5, 6, 7):
            self.landed(self.frm_sib[k], 7 + k)

    def sent(self):
        for copy in self.started:
            copy.wait_send()


class Swap:
    def __init__(self, me, buf, send, recv):
        self.me, self.buf, self.send, self.recv = me, buf, send, recv
        self.started = []

    def start(self):
        for i in (2, 6, 10, 14, 1, 3, 5, 7, 9, 11, 13, 15, 4, 8, 12):
            copy = rem_copy(
                self.buf.at[self.me],
                self.buf.at[self.me],
                self.send.at[i],
                self.recv.at[i],
                {"tm": lax.rem(self.me + i, N)},
            )
            copy.start()
            self.started.append(copy)

    def finish(self):
        for i in range(1, N):
            ref = self.buf.at[lax.rem(self.me + N - i, N)]
            rem_copy(ref, ref, self.send.at[i], self.recv.at[i], {"tm": self.me}).wait_recv()
        for copy in self.started:
            copy.wait_send()


def own_stats(x):
    mean = jnp.mean(x, axis=0, keepdims=True)
    dev = x - mean
    return mean, jnp.sum(dev * dev, axis=0, keepdims=True)


def joined_stats(buf):
    means = buf[:, 0, :]
    squares = buf[:, 1, :]
    mean = jnp.mean(means, axis=0, keepdims=True)
    dev = means - mean
    total = jnp.sum(squares, axis=0, keepdims=True) + HD * jnp.sum(dev * dev, axis=0, keepdims=True)
    return mean, lax.rsqrt(total * (1.0 / (N * HD)) + EPS)


def core_kernel(
    q_in, k_ref, v_ref, f_in, wg_in, wo_in, cot_ref, taps_ref, ng_ref, cg_ref,
    glu_out, out_out, taps_out,
    kv_own, qf_own, kv, qf, k_rows, v_cols, mixed, stats_a, stats_b, stats_z, stats_e,
    w_own, w_got, u_all, cot_all, small, taps_own, p, ds, y_pad, dz_pad, z_cols, g_cols, s_cols, dp,
    t_own, g_own, o_own, g_got, o_got, t_got, g_red, o_red, g_fin, o_fin,
    kv_s, kv_r, qf_s, qf_r, w_s, w_r, st_s, st_r, sz_s, sz_r, se_s, se_r,
    sb_s, sb_r, c_s, c_r, ua_s, ua_r, ub_s, ub_r, g1_s, g1_r, o1_s, o1_r, t1_s, t1_r, g2_s, g2_r, o2_s, o2_r, wx_s, wx_r, g3_s, g3_r, load_sem, own_sem,
    q_ref, f_ref, wg_ref, wo_ref,
):
    d = lax.axis_index("dp")
    t = lax.axis_index("tm")
    rows = k_ref.shape[0]
    length = mixed.shape[1]
    kernel = taps_ref.shape[0]
    half = kernel // 2
    y_at = t // 4
    group = lax.rem(t, 4)
    place = lambda block: lax.rem(block, 4) * 4 + block // 4

    barrier = pltpu.get_barrier_semaphore()

    def greet(dp_at, tm_at):
        pl.semaphore_signal(
            barrier, inc=1, device_id={"dp": dp_at, "tm": tm_at}, device_id_type=MESH
        )

    for i in range(1, N):
        greet(d, lax.rem(t + i, N))
        greet(lax.rem(d + i, N), t)
        greet(lax.rem(d + i, N), d)
        greet(t, lax.rem(t + i, N))

    @pl.when(t != d)
    def _():
        greet(d, d)
        greet(t, t)

    def turn_into(ref, buf, a):
        turned = jnp.transpose(ref[...])
        for j in range(N):
            buf[j, a * HD : (a + 1) * HD, :] = turned[j * HD : (j + 1) * HD]

    sent = []

    def scatter(src, dst, slot, send, recv):
        for i in range(1, N):
            peer = lax.rem(t + i, N)
            copy = rem_copy(src.at[peer], dst.at[slot], send.at[i], recv.at[i], {"tm": peer})
            copy.start()
            sent.append(copy)

    def arrived(dst, slot, i, send, recv):
        ref = dst.at[slot]
        rem_copy(ref, ref, send.at[i], recv.at[i], {"tm": t}).wait_recv()

    loads = [
        pltpu.make_async_copy(src, dst, load_sem.at[i])
        for i, (src, dst) in enumerate(
            ((q_in, q_ref), (f_in, f_ref), (wg_in, wg_ref), (wo_in, wo_ref))
        )
    ]
    for load in loads:
        load.start()
    turn_into(k_ref, kv_own, 0)
    turn_into(v_ref, kv_own, 1)
    cot_keep = pltpu.make_async_copy(cot_ref, cot_all.at[t], own_sem)
    cot_keep.start()
    pl.semaphore_wait(barrier, jnp.where(t == d, 4 * (N - 1), 4 * (N - 1) + 2))
    scatter(kv_own, kv, t, kv_s, kv_r)
    for load in loads:
        load.wait()
    turn_into(q_ref, qf_own, 0)
    turn_into(f_ref, qf_own, 1)
    scatter(qf_own, qf, t, qf_s, qf_r)
    cot = Gather(t, cot_ref, cot_all, lambda block: block, c_s, c_r)
    cot.start_near()
    width = N * HD
    for j in range(N):
        w_own[j] = jnp.concatenate(
            [
                wg_ref[:, j * HD : (j + 1) * HD],
                wg_ref[:, width + j * HD : width + (j + 1) * HD],
            ],
            axis=1,
        )
    x_at = d // 4
    for i in range(1, N):
        peer = lax.rem(t + i, N)

        @pl.when(x_at == y_at)
        def _():
            rem_copy(
                w_own.at[peer], w_got.at[y_at, group], w_s.at[i], w_r.at[group], {"tm": peer}
            ).start()

    kv[t] = kv_own[t]
    qf[t] = qf_own[t]

    @pl.when(x_at == y_at)
    def _():
        w_got[y_at, group] = w_own[t]


    small[...] = jnp.transpose(
        jnp.concatenate(
            [
                taps_ref[...],
                ng_ref[...].reshape(1, width),
                cg_ref[...].reshape(1, width),
                jnp.zeros((128 - kernel - 2, width), F32),
            ],
            axis=0,
        )
    )
    mine = small[pl.ds(pl.multiple_of(t * HD, HD), HD), :]
    lanes = taps_own.shape[1]
    blank = jnp.zeros((lanes - HD, 128), F32)
    taps_own[...] = jnp.transpose(jnp.concatenate([mine, blank], axis=0))[0:kernel]
    norm_gain = mine[:, kernel : kernel + 1]
    conv_gain = mine[:, kernel + 1 : kernel + 2]
    edge = jnp.zeros((half, lanes), F32)
    for pad in (y_pad, dz_pad):
        pad[0:half, :] = edge
        pad[length + half : length + 2 * half, :] = edge

    for i in range(1, N):
        arrived(kv, lax.rem(t + N - i, N), i, kv_s, kv_r)
    for s in range(N):
        k_rows[s * rows : (s + 1) * rows, :] = jnp.transpose(kv[s, 0:HD, :])
        v_cols[:, s * rows : (s + 1) * rows] = kv[s, HD : 2 * HD, :]
    factor = HD ** -0.5 * 1.4426950408889634
    pair = 2
    middle = length // 2

    def attend(low, high, h, stats):
        @pl.loop(low, high)
        def _(i):
            for j in range(pair):
                s = i * pair + j

                @pl.when(s != t)
                def _():
                    arrived(qf, s, lax.rem(t + N - s, N), qf_s, qf_r)

            queries = jnp.concatenate([qf[i * pair + j, 0:HD, :] for j in range(pair)], axis=1)
            field = jnp.concatenate([qf[i * pair + j, HD : 2 * HD, :] for j in range(pair)], axis=1)
            scores = jnp.dot(k_rows[...], queries, preferred_element_type=F32)
            top = jnp.max(scores, axis=0, keepdims=True)
            expo = jnp.exp2(scores * factor - top * factor)
            total = jnp.sum(expo, axis=0, keepdims=True)
            summed = jnp.dot(v_cols[...], expo.astype(BF16), preferred_element_type=F32)
            attention = (summed / total).astype(BF16)
            block = field.astype(F32) + attention.astype(F32)
            span = pair * rows
            mixed[:, pl.ds(pl.multiple_of(i * span, span), span)] = block
            cols = pl.ds(pl.multiple_of((i - h * (middle // span)) * span, span), span)
            mean, square = own_stats(block)
            stats[t, 0:1, cols] = mean
            stats[t, 1:2, cols] = square

    def make_u(h, stats, send, recv):
        mean, inv = joined_stats(stats)
        v = mixed[:, h * middle : (h + 1) * middle]
        u_all[h, place(t)] = ((v - mean) * inv * norm_gain).astype(BF16)
        gather = Gather(t, u_all.at[h, place(t)], u_all.at[h], place, send, recv)
        gather.start()
        return gather

    attend(0, 4, 0, stats_a)
    swap_a = Swap(t, stats_a, st_s, st_r)
    swap_a.start()
    attend(4, 6, 1, stats_b)
    swap_a.finish()
    ua = make_u(0, stats_a, ua_s, ua_r)
    attend(6, 8, 1, stats_b)
    swap_b = Swap(t, stats_b, sb_s, sb_r)
    swap_b.start()
    for g in range(4):

        @pl.when(x_at * 4 + g != t)
        def _():
            ref = w_got.at[x_at, g]
            rem_copy(ref, ref, w_s.at[0], w_r.at[g], {"tm": t}).wait_recv()

    for i in range(1, 4):
        ref = w_got.at[x_at]
        copy = rem_copy(
            ref, ref, wx_s.at[i], wx_r.at[i], {"dp": lax.rem(d + 4 * i, N), "tm": t}
        )
        copy.start()
        sent.append(copy)
    swap_b.finish()
    ub = make_u(1, stats_b, ub_s, ub_r)
    ua.relay_far()
    ua.relay_near()
    cot.start_far()
    cot.relay_near()

    def back_rows(z):
        @pl.loop(0, 4)
        def _(yy):
            first = yy * 4 + z * 2
            block = cot_all[pl.ds(first, 2)].reshape(2 * rows, width)
            ds[:, pl.ds(pl.multiple_of(first * rows, 2 * rows), 2 * rows)] = lax.dot_general(
                wo_ref[...], block, (((1,), (1,)), ((), ())), preferred_element_type=F32
            )

    z_at = lax.rem(t // 2, 2)
    for i in range(1, 4):
        ref = w_got.at[lax.rem(x_at + 4 - i, 4)]
        rem_copy(ref, ref, wx_s.at[i], wx_r.at[i], {"tm": t}).wait_recv()
    chunk = 512

    def product(g, h, first):
        weights = w_got[:, pl.ds(g, 1)].reshape(4 * HD, 2 * HD)

        @pl.loop(0, middle // chunk)
        def _(i):
            cols = pl.ds(pl.multiple_of(i * chunk, chunk), chunk)
            part = u_all[h, pl.ds(g * 4, 4), :, cols].reshape(4 * HD, chunk)
            part = lax.dot_general(
                weights, part, (((0,), (0,)), ((), ())), preferred_element_type=F32
            )
            cols = pl.ds(pl.multiple_of(h * middle + i * chunk, chunk), chunk)
            p[:, cols] = part if first else p[:, cols] + part

    step = 128
    blocks = length // step

    def gate(low, high):
        @pl.loop(low, high)
        def _(i):
            cols = pl.ds(pl.multiple_of(i * step, step), step)
            y = p[0:HD, cols] * jax.nn.sigmoid(p[HD : 2 * HD, cols])
            y = y.astype(BF16).astype(F32)
            y_pad[pl.ds(pl.multiple_of(half + i * step, half), step), :] = jnp.transpose(
                jnp.concatenate([y, blank], axis=0)
            )

    def conv(low, high):
        @pl.loop(low, high)
        def _(i):
            start = pl.multiple_of(i * step, step)
            z = jnp.zeros((step, lanes), F32)
            for k in range(kernel):
                z = z + taps_own[k : k + 1, :] * y_pad[pl.ds(start + k, step), :]
            z = jnp.transpose(z)[0:HD]
            cols = pl.ds(start, step)
            z_cols[:, cols] = z
            mean, square = own_stats(z)
            stats_z[t, 0:1, cols] = mean
            stats_z[t, 1:2, cols] = square

    side = lax.rem(group + 1, 2) - lax.rem(group, 2)
    other = lax.rem(group + 2, 4)
    product(group, 0, True)
    ua.near_from_sibling()
    product(group + side, 0, False)
    ub.relay_far()
    ub.relay_near()
    ua.relay_rest()
    cot.relay_far()
    cot.near_from_sibling()
    cot_keep.wait()
    back_rows(z_at)
    product(other, 0, False)
    ua.rest_from_sibling()
    product(other + side, 0, False)
    gate(0, blocks // 2)
    product(group, 1, True)
    ub.near_from_sibling()
    product(group + side, 1, False)
    conv(0, blocks // 2 - 1)
    ub.relay_rest()
    product(other, 1, False)
    ub.rest_from_sibling()
    product(other + side, 1, False)
    gate(blocks // 2, blocks)
    conv(blocks // 2 - 1, blocks)

    swap = Swap(t, stats_z, sz_s, sz_r)
    swap.start()
    cot.relay_rest()
    cot.rest_from_sibling()
    back_rows(1 - z_at)
    swap.finish()
    mean, inv = joined_stats(stats_z)
    zhat = (z_cols[...] - mean) * inv
    z_cols[...] = zhat
    n = zhat * conv_gain
    sgate = jax.nn.sigmoid(n)
    s_cols[...] = (n * sgate).astype(BF16)
    e = ds[...] * sgate * (1.0 + n * (1.0 - sgate)) * conv_gain
    g_cols[...] = e
    stats_e[t, 0:1, :] = jnp.sum(e, axis=0, keepdims=True)
    stats_e[t, 1:2, :] = jnp.sum(e * zhat, axis=0, keepdims=True)
    swap_e = Swap(t, stats_e, se_s, se_r)
    swap_e.start()

    for j in range(4):
        cols = slice(j * 4 * HD, (j + 1) * 4 * HD)
        part = jnp.dot(
            s_cols[...], cot_all[:, :, cols].reshape(length, 4 * HD), preferred_element_type=F32
        ).astype(BF16)
        for k in range(4):
            o_own[4 * j + k] = part[:, k * HD : (k + 1) * HD]
    for i in range(1, N):
        peer = lax.rem(d + i, N)
        copy = rem_copy(o_own.at[peer], o_got.at[d], o1_s.at[i], o1_r.at[i], {"dp": peer, "tm": t})
        copy.start()
        sent.append(copy)
    o_got[d] = o_own[d]

    swap_e.finish()
    sums = jnp.sum(stats_e[...], axis=0) * (1.0 / (N * HD))
    g_cols[...] = (
        ((g_cols[...] - sums[0:1] - z_cols[...] * sums[1:2]) * inv).astype(BF16).astype(F32)
    )

    @pl.loop(0, blocks)
    def turn(i):
        cols = pl.ds(pl.multiple_of(i * step, step), step)
        dz_pad[pl.ds(pl.multiple_of(half + i * step, half), step), :] = jnp.transpose(
            jnp.concatenate([g_cols[:, cols], blank], axis=0)
        )

    @pl.loop(0, blocks)
    def back(i):
        start = pl.multiple_of(i * step, step)
        dy = jnp.zeros((step, lanes), F32)
        for k in range(kernel):
            dy = dy + taps_own[k : k + 1, :] * dz_pad[pl.ds(start + 2 * half - k, step), :]
        dy = jnp.transpose(dy)[0:HD]
        cols = pl.ds(start, step)
        pa = p[0:HD, cols]
        sig = jax.nn.sigmoid(p[HD : 2 * HD, cols])
        dp[0:HD, cols] = (dy * sig).astype(BF16)
        dp[HD : 2 * HD, cols] = (dy * pa * sig * (1.0 - sig)).astype(BF16)

    @pl.loop(0, 4)
    def grads(i):
        g = lax.rem(i + d, 4)
        part = [
            lax.dot_general(
                u_all[h, pl.ds(g * 4, 4)].reshape(4 * HD, middle),
                dp[:, h * middle : (h + 1) * middle],
                (((1,), (1,)), ((), ())),
                preferred_element_type=F32,
            )
            for h in range(2)
        ]
        part = (part[0] + part[1]).astype(BF16)
        for j in range(4):
            block = part[j * HD : (j + 1) * HD]
            owner = 4 * j + g
            g_own[owner, 0:HD, :] = block[:, 0:128]
            g_own[owner, HD : HD + HD // 2, :] = jnp.concatenate(
                [block[0 : HD // 2, 128:], block[HD // 2 :, 128:]], axis=1
            )

            @pl.when(owner != d)
            def _():
                rem_copy(
                    g_own.at[owner], g_got.at[d], g1_s.at[owner], g1_r.at[d], {"dp": owner, "tm": t}
                ).start()

    g_got[d] = g_own[d]
    t_own[...] = jnp.zeros_like(t_own)

    @pl.loop(0, blocks)
    def tap_grads(i):
        start = pl.multiple_of(i * step, step)
        dz = dz_pad[pl.ds(pl.multiple_of(half + start, half), step), :]
        for k in range(kernel):
            prod = dz * y_pad[pl.ds(start + k, step), :]
            t_own[k : k + 1, :] += jnp.sum(prod, axis=0, keepdims=True)

    t_got[d] = t_own[...].astype(BF16)
    for i in range(1, N):
        peer = lax.rem(d + i, N)
        copy = rem_copy(t_got.at[d], t_got.at[d], t1_s.at[i], t1_r.at[i], {"dp": peer, "tm": t})
        copy.start()
        sent.append(copy)

    here = {"dp": d, "tm": t}

    def dp_arrived(buf, slot, send, recv, i):
        ref = buf.at[slot]
        rem_copy(ref, ref, send.at[i], recv.at[i], here).wait_recv()

    for i in range(1, N):
        slot = lax.rem(d + i, N)
        dp_arrived(g_got, slot, g1_s, g1_r, slot)
    g_red[...] = jnp.sum(g_got[...].astype(F32), axis=0).astype(BF16)
    g_slot = g_fin.at[t]
    for i in range(4):
        at_dp = y_at * 4 + lax.rem(d + i, 4)

        @pl.when(jnp.logical_or(t != d, at_dp != d))
        def _():
            rem_copy(g_red, g_slot, g2_s.at[i], g2_r.at[group], {"dp": at_dp, "tm": d}).start()

    @pl.when(t == d)
    def _():
        g_fin[t] = g_red[...]

    for k in range(4):
        s = x_at * 4 + k

        @pl.when(jnp.logical_or(s != t, t != d))
        def _():
            dp_arrived(g_fin, s, g2_s, g2_r, k)

    mine = g_fin.at[pl.ds(x_at * 4, 4)]
    for i in (1, 3, 2):
        copy = rem_copy(
            mine, mine, g3_s.at[i], g3_r.at[i], {"dp": lax.rem(d + 4 * i, N), "tm": t}
        )
        copy.start()
        sent.append(copy)

    for i in range(1, N):
        dp_arrived(o_got, lax.rem(d + N - i, N), o1_s, o1_r, i)
    o_red[...] = jnp.sum(o_got[...].astype(F32), axis=0).astype(BF16)
    for i in range(1, N):
        peer = lax.rem(d + i, N)
        copy = rem_copy(o_red, o_fin.at[d], o2_s.at[i], o2_r.at[i], {"dp": peer, "tm": t})
        copy.start()
        sent.append(copy)
    o_fin[d] = o_red[...]

    for i in range(1, N):
        dp_arrived(t_got, lax.rem(d + N - i, N), t1_s, t1_r, i)
        dp_arrived(o_fin, lax.rem(d + N - i, N), o2_s, o2_r, i)
    taps_out[...] = jnp.sum(t_got[...].astype(F32), axis=0)
    for j in range(4):
        out_out[:, j * 4 * HD : (j + 1) * 4 * HD] = jnp.concatenate(
            [o_fin[4 * j + k] for k in range(4)], axis=1
        )

    for i in (0, 1, 3, 2):
        j = lax.rem(x_at + 4 - i, 4)
        if i > 0:
            ref = g_fin.at[pl.ds(j * 4, 4)]
            rem_copy(ref, ref, g3_s.at[i], g3_r.at[i], here).wait_recv()
        first, second = [], []
        for k in range(4):
            s = 4 * j + k
            wide = g_fin[s, 0:HD, :]
            tail = g_fin[s, HD : HD + HD // 2, :]
            first.append(wide[:, 0:HD])
            second.append(wide[:, HD:])
            second.append(jnp.concatenate([tail[:, 0:64], tail[:, 64:]], axis=0))
        base = pl.multiple_of(j * 4 * HD, 4 * HD)
        glu_out[:, pl.ds(base, 4 * HD)] = jnp.concatenate(first, axis=1)
        base = pl.multiple_of(width + j * 4 * HD, 4 * HD)
        glu_out[:, pl.ds(base, 4 * HD)] = jnp.concatenate(second, axis=1)

    for i in range(4):
        at_dp = y_at * 4 + lax.rem(d + i, 4)

        @pl.when(jnp.logical_or(t != d, at_dp != d))
        def _():
            rem_copy(g_red, g_slot, g2_s.at[i], g2_r.at[group], here).wait_send()

    for copy in sent:
        copy.wait_send()
    for i in range(1, N):

        @pl.when(x_at == y_at)
        def _():
            ref = w_own.at[lax.rem(t + i, N)]
            rem_copy(ref, ref, w_s.at[i], w_r.at[group], {"tm": t}).wait_send()

    for i in range(1, N):
        owner = lax.rem(d + i, N)
        rem_copy(g_own.at[owner], g_got.at[d], g1_s.at[owner], g1_r.at[d], here).wait_send()
    cot.sent()
    ua.sent()
    ub.sent()


def anywhere():
    return pl.BlockSpec(memory_space=pl.ANY)


def vmem():
    return pl.BlockSpec(memory_space=pltpu.VMEM)


def core(query, keys, values, frames, w_glu, w_out, cot, taps, norm_gain, conv_gain):
    rows, width = query.shape
    length = rows * N
    kernel = taps.shape[0]
    lanes = 128
    packed = HD + HD // 2
    dma = pltpu.SemaphoreType.DMA
    V = pltpu.VMEM
    return pl.pallas_call(
        core_kernel,
        out_shape=(
            jax.ShapeDtypeStruct((HD, 2 * width), BF16),
            jax.ShapeDtypeStruct((HD, width), BF16),
            jax.ShapeDtypeStruct((kernel, lanes), F32),
        ),
        in_specs=[anywhere(), vmem(), vmem()] + [anywhere()] * 4 + [vmem()] * 3,
        out_specs=(vmem(), vmem(), vmem()),
        scratch_shapes=[
            V((N, 2 * HD, rows), BF16),
            V((N, 2 * HD, rows), BF16),
            V((N, 2 * HD, rows), BF16),
            V((N, 2 * HD, rows), BF16),
            V((length, HD), BF16),
            V((HD, length), BF16),
            V((HD, length), F32),
            V((N, 2, length // 2), F32),
            V((N, 2, length // 2), F32),
            V((N, 2, length), F32),
            V((N, 2, length), F32),
            V((N, HD, 2 * HD), BF16),
            V((4, 4, HD, 2 * HD), BF16),
            V((2, N, HD, length // 2), BF16),
            V((N, rows, width), BF16),
            V((width, 128), F32),
            V((kernel, lanes), F32),
            V((2 * HD, length), F32),
            V((HD, length), F32),
            V((length + kernel, lanes), F32),
            V((length + kernel, lanes), F32),
            V((HD, length), F32),
            V((HD, length), F32),
            V((HD, length), BF16),
            V((2 * HD, length), BF16),
            V((kernel, lanes), F32),
            V((N, packed, 128), BF16),
            V((N, HD, HD), BF16),
            V((N, packed, 128), BF16),
            V((N, HD, HD), BF16),
            V((N, kernel, lanes), BF16),
            V((packed, 128), BF16),
            V((HD, HD), BF16),
            V((N, packed, 128), BF16),
            V((N, HD, HD), BF16),
        ]
        + [dma((N,))] * 14
        + [dma((15,))] * 6
        + [dma((N,))] * 10
        + [dma((4,))] * 5
        + [dma(())]
        + [
            V((rows, width), BF16),
            V((rows, width), BF16),
            V((HD, 2 * width), BF16),
            V((HD, width), BF16),
        ],
        compiler_params=pltpu.CompilerParams(
            collective_id=0, has_side_effects=True, vmem_limit_bytes=58 * 2**20
        ),
        name="core",
    )(query, keys, values, frames, w_glu, w_out, cot, taps, norm_gain, conv_gain)


def local(frames, query, keys, values, norm_gain, conv_gain, w_glu, taps, w_out, cotangent):
    glu_grad, out_grad, taps_grad = core(
        query[0], keys[0], values[0], frames[0], w_glu, w_out, cotangent[0], taps,
        norm_gain, conv_gain,
    )
    return glu_grad.astype(F32), taps_grad[:, :HD], out_grad.astype(F32)


def solution(mesh):
    return jax.shard_map(
        local,
        mesh=mesh,
        in_specs=(
            P("dp", "tm", None),
            P("dp", "tm", None),
            P("dp", "tm", None),
            P("dp", "tm", None),
            P(),
            P(),
            P("tm", None),
            P(),
            P("tm", None),
            P("dp", "tm", None),
        ),
        out_specs=(P("tm", None), P(None, "tm"), P("tm", None)),
        check_vma=False,
    )
```
